256 devices in a mesh: wide: 32 (over y_hi, z, core), narrow: 8 (over y_lo, x).
Axes of the slice: x: 4, y: 4 (y_hi: 2, y_lo: 2; y = y_hi * 2 + y_lo), z: 8, core: 2. Of those that a mesh axis runs over, the one named last changes fastest.
Arguments:
- student_picture_vectors: bfloat16 [1152, 16384], P('narrow', 'wide'), may hold values from -52 to 52
- student_caption_vectors: bfloat16 [1152, 16384], P('narrow', 'wide'), may hold values from -52 to 52
- teacher_picture_vectors: bfloat16 [1152, 16384], P('narrow', 'wide'), may hold values from -52 to 52
- teacher_caption_vectors: bfloat16 [1152, 16384], P('narrow', 'wide'), may hold values from -52 to 52
- sharpness_factors: float32 [2], replicated, may hold values from 8 to 130, as said below
- offset_couple: float32 [2], replicated, may hold values from -17 to -7, as said below
Outputs:
- image_losses: float32 [2, 16384], P(None, ('wide', 'narrow'))
- text_losses: float32 [2, 16384], P(None, ('wide', 'narrow'))
The draws below stay inside these ranges and needn't reach their ends.
Inputs may be any that keep to these rules, and one draw needn't show every extreme that they name: `sharpness_factors`: entry 0 lies in 8 to 14, entry 1 in 90 to 130. `offset_couple`: entry 0 lies in -9 to -7, entry 1 in -17 to -12.
All inputs are finite; a program needn't handle non-finite values.
Results may differ from the reference program's by a relative error of at most 0.0003.
Values may be sent and summed in bfloat16 or wider, within the bound.
No kernel may reach another device: no remote copies, remote signals or barrier semaphores. Data moves between devices by JAX's collectives and lax.ppermute only.
A program may use at most 64 MiB of HBM per device.

```python
import math
import jax
import jax.numpy as jnp
from jax import lax

D = 1152
ROWS_DEV = 512
PAIRS = 16384
N_WIDE = 32


group_total = 48


def pair_content(key):
    content = jax.random.normal(jax.random.fold_in(key, 101), (PAIRS, D), jnp.float32)
    group_ids = jax.random.randint(jax.random.fold_in(key, 103), (PAIRS,), 0, group_total)
    centers = jax.random.normal(jax.random.fold_in(key, 104), (group_total, D), jnp.float32)
    shared = jnp.take(jnp.clip(centers, -4.0, 4.0), group_ids, axis=0)
    return (jnp.clip(content, -4.0, 4.0), shared)


def compose(key, content, shared, spread, lean, noise):
    log_scale = jax.random.uniform(jax.random.fold_in(key, 7), (PAIRS, 1), jnp.float32, 0.0, math.log(4.0))
    mixed = content + spread * noise + lean * shared
    return (jnp.exp(log_scale) * mixed).T.astype(jnp.bfloat16)


def own_noise(key):
    normal_part = jnp.clip(jax.random.normal(key, (PAIRS, D), jnp.float32), -4.0, 4.0)
    return normal_part


def draw_student_picture_vectors(key, part):
    content, shared = pair_content(key)
    key = jax.random.fold_in(key, 1)
    return compose(key, content, shared, 0.8, 0.8, own_noise(key))


def draw_student_caption_vectors(key, part):
    content, shared = pair_content(key)
    key = jax.random.fold_in(key, 2)
    return compose(key, content, shared, 0.8, 0.8, own_noise(key))


def draw_teacher_picture_vectors(key, part):
    content, shared = pair_content(key)
    key = jax.random.fold_in(key, 3)
    return compose(key, content, shared, 1.2, 0.3, own_noise(key))


def draw_teacher_caption_vectors(key, part):
    content, shared = pair_content(key)
    key = jax.random.fold_in(key, 4)
    return compose(key, content, shared, 1.2, 0.3, own_noise(key))


def draw_sharpness_factors(key, part):
    key = jax.random.fold_in(key, 5)
    lower = jnp.array([math.log(8.0), math.log(90.0)], jnp.float32)
    upper = jnp.array([math.log(14.0), math.log(130.0)], jnp.float32)
    fraction = jax.random.uniform(key, (2,), jnp.float32, 0.0, 1.0)
    return jnp.exp(lower + fraction * (upper - lower)).astype(jnp.float32)


def draw_offset_couple(key, part):
    key = jax.random.fold_in(key, 6)
    lower = jnp.array([-9.0, -17.0], jnp.float32)
    upper = jnp.array([-7.0, -12.0], jnp.float32)
    fraction = jax.random.uniform(key, (2,), jnp.float32, 0.0, 1.0)
    return (lower + fraction * (upper - lower)).astype(jnp.float32)


def setup_inputs(seed: int = 0) -> dict:
    seeds = jax.random.split(jax.random.key(seed), 7)
    return {
        "student_picture_vectors": draw_student_picture_vectors(jax.random.fold_in(seeds[6], 71), 0),
        "student_caption_vectors": draw_student_caption_vectors(jax.random.fold_in(seeds[6], 71), 0),
        "teacher_picture_vectors": draw_teacher_picture_vectors(jax.random.fold_in(seeds[6], 71), 0),
        "teacher_caption_vectors": draw_teacher_caption_vectors(jax.random.fold_in(seeds[6], 71), 0),
        "sharpness_factors": draw_sharpness_factors(jax.random.fold_in(seeds[6], 71), 0),
        "offset_couple": draw_offset_couple(jax.random.fold_in(seeds[6], 71), 0),
    }


epsilon = 1e-06

def network_aggregates(image_cols, text_cols, temper, offset):
    image_rows = image_cols.T
    text_rows = text_cols.T
    image_scale = lax.rsqrt(lax.optimization_barrier(jnp.sum(jnp.square(image_rows.astype(jnp.float32)), axis=1)) + epsilon)
    text_scale = lax.rsqrt(lax.optimization_barrier(jnp.sum(jnp.square(text_rows.astype(jnp.float32)), axis=1)) + epsilon)
    text_index = jnp.arange(PAIRS, dtype=jnp.int32)

    def block_step(column_total, block_number):
        first = (block_number * ROWS_DEV).astype(jnp.int32)
        image_block = lax.dynamic_slice_in_dim(image_rows, first, ROWS_DEV, 0)
        scale_block = lax.dynamic_slice_in_dim(image_scale, first, ROWS_DEV, 0)
        products = jnp.dot(image_block, text_rows.T, preferred_element_type=jnp.float32)
        cosine = products * scale_block[:, None] * text_scale[None, :]
        logits = temper * cosine + offset
        image_index = first + jnp.arange(ROWS_DEV, dtype=jnp.int32)
        matched = image_index[:, None] == text_index[None, :]
        losses = jax.nn.softplus(jnp.where(matched, -logits, logits))
        return (column_total + lax.optimization_barrier(jnp.sum(losses, axis=0)), lax.optimization_barrier(jnp.sum(losses, axis=1)))
    start_total = jnp.zeros((PAIRS,), jnp.float32)
    column_total, row_blocks = lax.scan(block_step, start_total, jnp.arange(N_WIDE, dtype=jnp.int32))
    return (row_blocks.reshape(PAIRS), column_total)

def reference(student_picture_vectors, student_caption_vectors, teacher_picture_vectors, teacher_caption_vectors, sharpness_factors, offset_couple):
    student_picture_totals, student_caption_totals = network_aggregates(student_picture_vectors, student_caption_vectors, sharpness_factors[0], offset_couple[0])
    teacher_picture_totals, teacher_caption_totals = network_aggregates(teacher_picture_vectors, teacher_caption_vectors, sharpness_factors[1], offset_couple[1])
    return (jnp.stack([student_picture_totals, teacher_picture_totals]), jnp.stack([student_caption_totals, teacher_caption_totals]))
```

```python
import functools

import jax
import jax.numpy as jnp
from jax import lax
from jax.experimental import pallas as pl
from jax.experimental.pallas import tpu as pltpu
from jax.sharding import PartitionSpec as P

epsilon = 1e-06
AXES = ("wide", "narrow")
X, LO, HI, Z, CORES = 4, 2, 2, 8, 2
NARROW = LO * X


def device(hi, z, core, lo, x):
    return ((hi * Z + z) * CORES + core) * NARROW + lo * X + x


def places():
    for hi in range(HI):
        for z in range(Z):
            for core in range(CORES):
                for lo in range(LO):
                    for x in range(X):
                        yield hi, z, core, lo, x


def send(value, step):
    pairs = [(place, step(*place)) for place in places()]
    pairs = [(device(*place), device(*target)) for place, target in pairs if target]
    return lax.ppermute(value, AXES, pairs)


def send_core(value):
    return send(value, lambda hi, z, core, lo, x: (hi, z, core ^ 1, lo, x))


def send_first(value, d):
    return send(
        value,
        lambda hi, z, core, lo, x: (
            (hi ^ (d >> 1), z, core, lo ^ (d & 1), x) if core else (hi, z, core, lo, x ^ d)
        ),
    )


def send_second(value, d):
    return send(
        value,
        lambda hi, z, core, lo, x: (
            (hi, z, core, lo, x ^ d) if core else (hi ^ (d >> 1), z, core, lo ^ (d & 1), x)
        ),
    )


def groups_by(key, order):
    groups = {}
    for place in places():
        groups.setdefault(key(*place), []).append(place)
    return [
        [device(*place) for place in sorted(group, key=lambda place: order(*place))]
        for group in groups.values()
    ]


def exchange(value, groups):
    return lax.all_to_all(value, AXES, 0, 0, axis_index_groups=groups, tiled=True)


def send_z(value, dz):
    return send(value, lambda hi, z, core, lo, x: (hi, (z + dz) % Z, core, lo, x))


VMEM = pl.BlockSpec(memory_space=pltpu.VMEM)
SMEM = pl.BlockSpec(memory_space=pltpu.SMEM)
LARGE = 60 * 1024 * 1024
SMALL = pltpu.CompilerParams(vmem_limit_bytes=4 * 1024 * 1024)


FOLD = 80


def start_kernel(p0, p1, c0, c1, own_ref, give_ref, out_ref):
    core = lax.axis_index("wide") % CORES
    give_ref[...] = jnp.where(core == 0, p1[...], p0[...])
    own_ref[...] = jnp.where(core == 0, p0[...], p1[...])
    features, block = c0.shape
    share = block // NARROW
    for model, ref in enumerate((c0, c1)):
        for n in range(NARROW):
            piece = ref[:, n * share : (n + 1) * share]
            rest = jnp.concatenate(
                [piece[FOLD:], jnp.zeros((2 * FOLD - features, share), piece.dtype)], axis=0
            )
            out_ref[model * NARROW + n] = jnp.concatenate([piece[:FOLD], rest], axis=1)


def start(pictures, captions):
    features, block = captions[0].shape
    dtype = captions[0].dtype
    return pl.pallas_call(
        start_kernel,
        in_specs=[VMEM] * 4,
        out_specs=[VMEM] * 3,
        out_shape=[
            jax.ShapeDtypeStruct((features, block), dtype),
            jax.ShapeDtypeStruct((features, block), dtype),
            jax.ShapeDtypeStruct((CORES * NARROW, FOLD, 2 * block // NARROW), dtype),
        ],
        compiler_params=pltpu.CompilerParams(vmem_limit_bytes=LARGE),
    )(*pictures, *captions)


def rows_kernel(place, in_ref, out_ref):
    features = out_ref.shape[1] // NARROW
    share = out_ref.shape[0] // CORES
    columns = []
    for other in range(CORES):
        parts = []
        for slot in range(NARROW):
            piece = in_ref[(place[2] ^ other) * NARROW + (place[0] ^ slot)]
            parts += [piece[:, :share], piece[: features - FOLD, share:]]
        columns.append(jnp.concatenate(parts, axis=0))
    out_ref[...] = jnp.concatenate(columns, axis=1).T


def text_rows(place, shares, features):
    return pl.pallas_call(
        rows_kernel,
        in_specs=[SMEM, VMEM],
        out_specs=VMEM,
        out_shape=jax.ShapeDtypeStruct((shares.shape[2], NARROW * features), shares.dtype),
        compiler_params=SMALL,
    )(place, shares)


def softplus(value):
    power = jnp.exp2(jnp.abs(value) * -1.4426950408889634)
    near = 1.0 + power
    return jnp.maximum(value, 0.0) + (jnp.log(near) + (power - (near - 1.0)))


def pair_kernel(sharpness, offsets, place, *refs, texts, first):
    text_refs, refs = refs[:texts], refs[texts:]
    text, even, odd, text_scale, total = refs[-5:]
    if first:
        line, one, two_low, two_high, three, image_sums, text_sums, image, image_scale = refs[:9]
    else:
        image, image_scale, before_image, before_text, keep_out, give_out = refs[:6]
        image_sums, text_sums = refs[6:8]
    narrow, hi, core = place[0], place[1], place[2]
    low = narrow // X
    temper = jnp.where(core == 0, sharpness[0], sharpness[1])
    offset = jnp.where(core == 0, offsets[0], offsets[1])
    rows, depth = text.shape
    columns = image.shape[4]

    row = 0
    for ref in text_refs:
        size = ref.shape[0]
        text[row : row + size, :] = ref[...]
        row += size

    if first:

        @pl.when(core == 0)
        def _():
            for block in range(4):
                owner = block // 2
                if block % 2 == 0:
                    image[block, 0] = line[:, owner]
                    image[block, 1] = one[:, owner]
                else:
                    image[block, 0, 0:2] = two_low[:, owner]
                    image[block, 0, 2:4] = two_high[:, owner]
                    image[block, 1] = three[:, owner]

        @pl.when(core == 1)
        def _():
            for block in range(4):
                owner, at = block // 2, slice(block % 2 * 2, block % 2 * 2 + 2)
                two = two_high if block % 2 else two_low
                image[block, :, 0] = line[at, owner]
                image[block, :, 1] = one[at, owner]
                image[block, :, 2] = two[:, owner]
                image[block, :, 3] = three[at, owner]

    total[...] = jnp.zeros_like(total)

    @pl.loop(0, rows // 128)
    def _(i):
        at = pl.ds(pl.multiple_of(i * 128, 128), 128)
        squares = jnp.square(text[at, :].astype(jnp.float32))
        norm = jnp.sum(squares, axis=1, keepdims=True) + epsilon
        text_scale[at, :] = jnp.broadcast_to(temper * lax.rsqrt(norm), (128, 128))

    def scale_block(block):
        flat = image.at[block].reshape(depth, columns)
        norm = jnp.zeros((8, columns), jnp.float32)
        for r in range(0, depth, 32):
            part = jnp.square(flat[r : r + 32, :].astype(jnp.float32))
            norm += jnp.sum(part.reshape(4, 8, columns), axis=0)
        norm = jnp.sum(norm, axis=0, keepdims=True) + epsilon
        image_scale[block] = lax.rsqrt(norm)

    def product(block, out):
        flat = image.at[block].reshape(depth, columns)
        out[...] = jnp.dot(text[...], flat[...], preferred_element_type=jnp.float32)

    def losses(block, products):
        owner, high = block // 2, block % 2
        across = image_scale[block]
        image_total = jnp.zeros((8, columns), jnp.float32)
        step = 32
        for r in range(0, rows, step):
            at = slice(r, r + step)
            down = text_scale[at, :]
            down = jnp.concatenate([down] * (columns // 128), axis=1)
            logit = products[at, :] * down * across + offset
            if first and high == 0 and r < 128:
                mine = owner == (core ^ (r // 64))
                shift = jnp.where(mine, narrow * 64 + r % 64, -columns)
                i = lax.broadcasted_iota(jnp.int32, logit.shape, 0)
                j = lax.broadcasted_iota(jnp.int32, logit.shape, 1)
                logit = jnp.where(j - i == shift, -logit, logit)
            loss = softplus(logit)
            image_total += jnp.sum(loss.reshape(step // 8, 8, columns), axis=0)
            total[at, :] += sum(loss[:, lane : lane + 128] for lane in range(0, columns, 128))
        summed = jnp.sum(image_total, axis=0, keepdims=True)
        for j in range(columns // 128):
            row = (high * 2 + ((j // 2) ^ low)) * 4 + owner * 2 + j % 2
            lanes = summed[:, j * 128 : (j + 1) * 128]
            image_sums[pl.ds(row, 1), :] = lanes

    buffers = (even, odd)
    for block in range(5):
        if block < 4:
            if first:
                scale_block(block)
            product(block, buffers[block % 2])
        if block > 0:
            losses(block - 1, buffers[(block - 1) % 2])

    text_sums[...] = jnp.zeros_like(text_sums) if first else before_text[...]
    for i, planes in enumerate((0, 1, 7, 2, 6) if first else (3, 5, 4)):
        summed = jnp.sum(total[i * 128 : (i + 1) * 128, :].T, axis=0, keepdims=True)
        summed = jnp.where(core == 0, summed, pltpu.roll(summed, 64, 1))
        row = planes // 2 * 4 + planes % 2
        text_sums[row : row + 1, :] = summed
    if not first:
        images_all = image_sums[...] + before_image[...]
        keep_out[...] = jnp.where(core == 0, images_all, text_sums[...])
        give_out[...] = jnp.where(core == 0, text_sums[...], images_all)


def pair_sums(sharpness, offsets, place, texts, operands, first):
    rows = sum(text.shape[0] for text in texts)
    depth = texts[0].shape[1]
    features, columns = operands[0].shape[-2:]
    sums = jax.ShapeDtypeStruct((16, 128), jnp.float32)
    outs = [sums, sums]
    buffers = [
        pltpu.VMEM((rows, depth), jnp.bfloat16),
        pltpu.VMEM((rows, columns), jnp.float32),
        pltpu.VMEM((rows, columns), jnp.float32),
        pltpu.VMEM((rows, 128), jnp.float32),
        pltpu.VMEM((rows, 128), jnp.float32),
    ]
    if first:
        outs += [
            jax.ShapeDtypeStruct((4, LO, X, features, columns), jnp.bfloat16),
            jax.ShapeDtypeStruct((4, 1, columns), jnp.float32),
        ]
    else:
        buffers = [pltpu.VMEM((16, 128), jnp.float32)] * 2 + buffers
    operands = (*texts, *operands)
    return pl.pallas_call(
        functools.partial(pair_kernel, texts=len(texts), first=first),
        in_specs=[SMEM] * 3 + [VMEM] * len(operands),
        out_specs=[VMEM] * len(outs),
        out_shape=outs,
        scratch_shapes=buffers,
        compiler_params=pltpu.CompilerParams(vmem_limit_bytes=24 * 1024 * 1024),
        cost_estimate=pl.CostEstimate(
            flops=8 * rows * columns * depth,
            bytes_accessed=2 * depth * (rows + 4 * columns),
            transcendentals=8 * rows * columns,
        ),
    )(sharpness, offsets, place, *operands)


def spread_kernel(place, keep_ref, got_ref, out_ref):
    narrow, hi, core, z = place[0], place[1], place[2], place[3]
    y = hi * 2 + narrow // X
    out_ref[...] = jnp.zeros_like(out_ref)

    @pl.when(core == 0)
    def _():
        for model, ref in enumerate((keep_ref, got_ref)):
            for dy in range(HI * LO):
                for x in range(X):
                    row, lanes = dy * 4 + x // 2, slice(x % 2 * 64, x % 2 * 64 + 64)
                    out_ref[(y ^ dy) * X + x, model : model + 1, :] = jnp.concatenate(
                        [ref[row : row + 1, lanes], ref[row + 2 : row + 3, lanes]], axis=1
                    )

    @pl.when(core == 1)
    def _():
        for model, ref in enumerate((keep_ref, got_ref)):
            for planes in range(Z):
                row = planes // 2 * 4 + planes % 2
                to = lax.rem(z + Z - planes, Z)
                out_ref[to * HI + hi, model : model + 1, :] = ref[row : row + 1, :]


def last_kernel(place, mine_ref, got_ref, image_ref, text_ref):
    mine, got = jnp.sum(mine_ref[...], axis=0), jnp.sum(got_ref[...], axis=0)

    @pl.when(place[2] == 0)
    def _():
        image_ref[...] = mine[:, :64]
        text_ref[0:1, :] = got[1:2, :64]
        text_ref[1:2, :] = got[0:1, :64]

    @pl.when(place[2] == 1)
    def _():
        image_ref[...] = got[:, 64:]
        text_ref[0:1, :] = mine[1:2, 64:]
        text_ref[1:2, :] = mine[0:1, 64:]


def reduce_sums(place, keep, give):
    def part(*shape):
        return jax.ShapeDtypeStruct(shape, jnp.float32)

    def call(kernel, specs, outs, *operands):
        return pl.pallas_call(
            kernel,
            in_specs=specs,
            out_specs=[VMEM] * len(outs),
            out_shape=outs,
            compiler_params=SMALL,
        )(*operands)

    groups = groups_by(
        lambda hi, z, c, lo, x: (c, lo, x) if c else (c, z, 0),
        lambda hi, z, c, lo, x: (z, hi) if c else (hi, lo, x),
    )
    chunks = HI * LO * X
    (sums,) = call(
        spread_kernel, [SMEM, VMEM, VMEM], [part(chunks, 2, 128)], place, keep, send_core(give)
    )
    mine = exchange(sums, groups)
    got = send_core(mine)
    return call(last_kernel, [SMEM, VMEM, VMEM], [part(2, 64)] * 2, place, mine, got)


def on_device(
    student_picture_vectors,
    student_caption_vectors,
    teacher_picture_vectors,
    teacher_caption_vectors,
    sharpness_factors,
    offset_couple,
):
    features = student_picture_vectors.shape[0]
    narrow = lax.axis_index("narrow")
    wide = lax.axis_index("wide")
    core = wide % CORES
    place = jnp.stack([narrow, wide // (Z * CORES), core, wide // CORES % Z]).astype(jnp.int32)
    learner = core == 0

    own_pictures, pictures, shares = start(
        (student_picture_vectors, teacher_picture_vectors),
        (student_caption_vectors, teacher_caption_vectors),
    )

    by_row = groups_by(lambda hi, z, c, lo, x: (hi, z), lambda hi, z, c, lo, x: (c, lo, x))
    text = text_rows(place, exchange(shares, by_row), features)

    other_pictures = send_core(pictures)
    both = jnp.where(
        learner,
        jnp.stack([own_pictures, other_pictures]),
        jnp.stack([other_pictures, own_pictures]),
    )
    ring = [both] + [send_first(both, d) for d in (1, 2, 3)]
    _, *ring = lax.optimization_barrier((text, *ring))
    line = jnp.stack(ring)
    one, three = send_second(line, 1), send_second(line, 3)
    two_low, two_high = send_second(three[:2], 1), send_second(one[2:], 3)

    up1, down1 = send_z(text, 1), send_z(text, -1)
    up2, down2 = send_z(up1, 1), send_z(down1, -1)
    up3, down3 = send_z(up2, 1), send_z(down2, -1)
    middle = text.shape[0] // 2
    up4, down4 = send_z(up3[:middle], 1), send_z(down3[middle:], -1)

    scalars = (sharpness_factors, offset_couple, place)
    image_sums, text_sums, image, scale = pair_sums(
        *scalars, (text, up1, down1, up2, down2), (line, one, two_low, two_high, three), True
    )
    keep, give = pair_sums(
        *scalars, (up3, down3, up4, down4), (image, scale, image_sums, text_sums), False
    )
    return tuple(reduce_sums(place, keep, give))


def solution(mesh):
    return jax.shard_map(
        on_device,
        mesh=mesh,
        in_specs=(
            P("narrow", "wide"),
            P("narrow", "wide"),
            P("narrow", "wide"),
            P("narrow", "wide"),
            P(),
            P(),
        ),
        out_specs=(P(None, ("wide", "narrow")), P(None, ("wide", "narrow"))),
        check_vma=False,
    )
```

```python
import functools

import jax
import jax.numpy as jnp
from jax import lax
from jax.experimental import pallas as pl
from jax.experimental.pallas import tpu as pltpu
from jax.sharding import PartitionSpec as P

epsilon = 1e-06
AXES = ("wide", "narrow")
X, LO, HI, Z, CORES = 4, 2, 2, 8, 2
NARROW = LO * X


def device(hi, z, core, lo, x):
    return ((hi * Z + z) * CORES + core) * NARROW + lo * X + x


def places():
    for hi in range(HI):
        for z in range(Z):
            for core in range(CORES):
                for lo in range(LO):
                    for x in range(X):
                        yield hi, z, core, lo, x


def send(value, step):
    pairs = [(place, step(*place)) for place in places()]
    pairs = [(device(*place), device(*target)) for place, target in pairs if target]
    return lax.ppermute(value, AXES, pairs)


def send_core(value):
    return send(value, lambda hi, z, core, lo, x: (hi, z, core ^ 1, lo, x))


def send_first(value, d):
    return send(
        value,
        lambda hi, z, core, lo, x: (
            (hi ^ (d >> 1), z, core, lo ^ (d & 1), x) if core else (hi, z, core, lo, x ^ d)
        ),
    )


def send_second(value, d):
    return send(
        value,
        lambda hi, z, core, lo, x: (
            (hi, z, core, lo, x ^ d) if core else (hi ^ (d >> 1), z, core, lo ^ (d & 1), x)
        ),
    )


def groups_by(key, order):
    groups = {}
    for place in places():
        groups.setdefault(key(*place), []).append(place)
    return [
        [device(*place) for place in sorted(group, key=lambda place: order(*place))]
        for group in groups.values()
    ]


def exchange(value, groups):
    return lax.all_to_all(value, AXES, 0, 0, axis_index_groups=groups, tiled=True)


def send_z(value, dz):
    return send(value, lambda hi, z, core, lo, x: (hi, (z + dz) % Z, core, lo, x))


VMEM = pl.BlockSpec(memory_space=pltpu.VMEM)
SMEM = pl.BlockSpec(memory_space=pltpu.SMEM)
LARGE = 60 * 1024 * 1024
SMALL = pltpu.CompilerParams(vmem_limit_bytes=4 * 1024 * 1024)


FOLD = 80


def start_kernel(p0, p1, c0, c1, own_ref, give_ref, out_ref):
    core = lax.axis_index("wide") % CORES
    give_ref[...] = jnp.where(core == 0, p1[...], p0[...])
    own_ref[...] = jnp.where(core == 0, p0[...], p1[...])
    features, block = c0.shape
    share = block // NARROW
    for model, ref in enumerate((c0, c1)):
        for n in range(NARROW):
            piece = ref[:, n * share : (n + 1) * share]
            rest = jnp.concatenate(
                [piece[FOLD:], jnp.zeros((2 * FOLD - features, share), piece.dtype)], axis=0
            )
            out_ref[model * NARROW + n] = jnp.concatenate([piece[:FOLD], rest], axis=1)


def start(pictures, captions):
    features, block = captions[0].shape
    dtype = captions[0].dtype
    return pl.pallas_call(
        start_kernel,
        in_specs=[VMEM] * 4,
        out_specs=[VMEM] * 3,
        out_shape=[
            jax.ShapeDtypeStruct((features, block), dtype),
            jax.ShapeDtypeStruct((features, block), dtype),
            jax.ShapeDtypeStruct((CORES * NARROW, FOLD, 2 * block // NARROW), dtype),
        ],
        compiler_params=pltpu.CompilerParams(vmem_limit_bytes=LARGE),
    )(*pictures, *captions)


def rows_kernel(place, in_ref, out_ref):
    features = out_ref.shape[1] // NARROW
    share = out_ref.shape[0] // CORES
    columns = []
    for other in range(CORES):
        parts = []
        for slot in range(NARROW):
            piece = in_ref[(place[2] ^ other) * NARROW + (place[0] ^ slot)]
            parts += [piece[:, :share], piece[: features - FOLD, share:]]
        columns.append(jnp.concatenate(parts, axis=0))
    out_ref[...] = jnp.concatenate(columns, axis=1).T


def text_rows(place, shares, features):
    return pl.pallas_call(
        rows_kernel,
        in_specs=[SMEM, VMEM],
        out_specs=VMEM,
        out_shape=jax.ShapeDtypeStruct((shares.shape[2], NARROW * features), shares.dtype),
        compiler_params=SMALL,
    )(place, shares)


def tail_power(value):
    return jnp.exp2(jnp.abs(value) * -1.4426950408889634)


def both_tails(a, b):
    return (a + b) + a * b


def log_tail(tail):
    near = 1.0 + tail
    return jnp.log(near) + (tail - (near - 1.0))


def pair_kernel(sharpness, offsets, place, *refs, texts, first):
    text_refs, refs = refs[:texts], refs[texts:]
    text, even, odd, text_scale, total = refs[-5:]
    if first:
        line, one, two_low, two_high, three, image_sums, text_sums, image, image_scale = refs[:9]
    else:
        image, image_scale, before_image, before_text, keep_out, give_out = refs[:6]
        image_sums, text_sums = refs[6:8]
    narrow, hi, core = place[0], place[1], place[2]
    low = narrow // X
    temper = jnp.where(core == 0, sharpness[0], sharpness[1])
    offset = jnp.where(core == 0, offsets[0], offsets[1])
    rows, depth = text.shape
    columns = image.shape[4]

    row = 0
    for ref in text_refs:
        size = ref.shape[0]
        text[row : row + size, :] = ref[...]
        row += size

    if first:

        @pl.when(core == 0)
        def _():
            for block in range(4):
                owner = block // 2
                if block % 2 == 0:
                    image[block, 0] = line[:, owner]
                    image[block, 1] = one[:, owner]
                else:
                    image[block, 0, 0:2] = two_low[:, owner]
                    image[block, 0, 2:4] = two_high[:, owner]
                    image[block, 1] = three[:, owner]

        @pl.when(core == 1)
        def _():
            for block in range(4):
                owner, at = block // 2, slice(block % 2 * 2, block % 2 * 2 + 2)
                two = two_high if block % 2 else two_low
                image[block, :, 0] = line[at, owner]
                image[block, :, 1] = one[at, owner]
                image[block, :, 2] = two[:, owner]
                image[block, :, 3] = three[at, owner]

    total[...] = jnp.zeros_like(total)

    @pl.loop(0, rows // 128)
    def _(i):
        at = pl.ds(pl.multiple_of(i * 128, 128), 128)
        squares = jnp.square(text[at, :].astype(jnp.float32))
        norm = jnp.sum(squares, axis=1, keepdims=True) + epsilon
        text_scale[at, :] = jnp.broadcast_to(temper * lax.rsqrt(norm), (128, 128))

    def scale_block(block):
        flat = image.at[block].reshape(depth, columns)
        norm = jnp.zeros((8, columns), jnp.float32)
        for r in range(0, depth, 32):
            part = jnp.square(flat[r : r + 32, :].astype(jnp.float32))
            norm += jnp.sum(part.reshape(4, 8, columns), axis=0)
        norm = jnp.sum(norm, axis=0, keepdims=True) + epsilon
        image_scale[block] = lax.rsqrt(norm)

    span = even.shape[0]
    parts = rows // span

    def product(block, part, out):
        flat = image.at[block].reshape(depth, columns)
        out[...] = jnp.dot(
            text[part * span : (part + 1) * span, :],
            flat[...],
            preferred_element_type=jnp.float32,
        )

    def losses(block, part, products):
        owner, high = block // 2, block % 2
        across = image_scale[block]
        image_total = jnp.zeros((8, columns), jnp.float32)
        step = 32
        column_tail = None
        for r in range(0, span, step):
            at = slice(part * span + r, part * span + r + step)
            down = text_scale[at, :]
            down = jnp.concatenate([down] * (columns // 128), axis=1)
            logit = products[r : r + step, :] * down * across + offset
            if first and high == 0 and part == 0 and r < 128:
                mine = owner == (core ^ (r // 64))
                shift = jnp.where(mine, narrow * 64 + r % 64, -columns)
                i = lax.broadcasted_iota(jnp.int32, logit.shape, 0)
                j = lax.broadcasted_iota(jnp.int32, logit.shape, 1)
                logit = jnp.where(j - i == shift, -logit, logit)
            above = jnp.maximum(logit, 0.0)
            tail = tail_power(logit)
            tiles = [slice(lane, lane + 128) for lane in range(0, columns, 128)]
            row_tail = functools.reduce(both_tails, [tail[:, tile] for tile in tiles])
            total[at, :] += log_tail(row_tail) + sum(above[:, tile] for tile in tiles)
            for g in range(0, step, 8):
                group = tail[g : g + 8, :]
                column_tail = group if column_tail is None else both_tails(column_tail, group)
            image_total += jnp.sum(above.reshape(step // 8, 8, columns), axis=0)
            if r % 64 or r + step == span:
                image_total += log_tail(column_tail)
                column_tail = None
        summed = jnp.sum(image_total, axis=0, keepdims=True)
        for j in range(columns // 128):
            row = (high * 2 + ((j // 2) ^ low)) * 4 + owner * 2 + j % 2
            lanes = summed[:, j * 128 : (j + 1) * 128]
            if part == 0:
                image_sums[pl.ds(row, 1), :] = lanes
            else:
                image_sums[pl.ds(row, 1), :] += lanes

    steps = [(block, part) for block in range(4) for part in range(parts)]
    buffers = (even, odd)
    for n, step in enumerate(steps + [None]):
        if step is not None:
            if first and step[1] == 0:
                scale_block(step[0])
            product(*step, buffers[n % 2])
        if n > 0:
            losses(*steps[n - 1], buffers[(n - 1) % 2])

    text_sums[...] = jnp.zeros_like(text_sums) if first else before_text[...]
    for i, planes in enumerate((0, 1, 7, 2, 6) if first else (3, 5, 4)):
        summed = jnp.sum(total[i * 128 : (i + 1) * 128, :].T, axis=0, keepdims=True)
        summed = jnp.where(core == 0, summed, pltpu.roll(summed, 64, 1))
        row = planes // 2 * 4 + planes % 2
        text_sums[row : row + 1, :] = summed
    if not first:
        images_all = image_sums[...] + before_image[...]
        keep_out[...] = jnp.where(core == 0, images_all, text_sums[...])
        give_out[...] = jnp.where(core == 0, text_sums[...], images_all)


def pair_sums(sharpness, offsets, place, texts, operands, first):
    rows = sum(text.shape[0] for text in texts)
    depth = texts[0].shape[1]
    features, columns = operands[0].shape[-2:]
    sums = jax.ShapeDtypeStruct((16, 128), jnp.float32)
    outs = [sums, sums]
    span = rows // (4 if first else 3)
    buffers = [
        pltpu.VMEM((rows, depth), jnp.bfloat16),
        pltpu.VMEM((span, columns), jnp.float32),
        pltpu.VMEM((span, columns), jnp.float32),
        pltpu.VMEM((rows, 128), jnp.float32),
        pltpu.VMEM((rows, 128), jnp.float32),
    ]
    if first:
        outs += [
            jax.ShapeDtypeStruct((4, LO, X, features, columns), jnp.bfloat16),
            jax.ShapeDtypeStruct((4, 1, columns), jnp.float32),
        ]
    else:
        buffers = [pltpu.VMEM((16, 128), jnp.float32)] * 2 + buffers
    operands = (*texts, *operands)
    return pl.pallas_call(
        functools.partial(pair_kernel, texts=len(texts), first=first),
        in_specs=[SMEM] * 3 + [VMEM] * len(operands),
        out_specs=[VMEM] * len(outs),
        out_shape=outs,
        scratch_shapes=buffers,
        compiler_params=pltpu.CompilerParams(vmem_limit_bytes=24 * 1024 * 1024),
        cost_estimate=pl.CostEstimate(
            flops=8 * rows * columns * depth,
            bytes_accessed=2 * depth * (rows + 4 * columns),
            transcendentals=8 * rows * columns,
        ),
    )(sharpness, offsets, place, *operands)


def spread_kernel(place, keep_ref, got_ref, out_ref):
    narrow, hi, core, z = place[0], place[1], place[2], place[3]
    y = hi * 2 + narrow // X
    out_ref[...] = jnp.zeros_like(out_ref)

    @pl.when(core == 0)
    def _():
        for model, ref in enumerate((keep_ref, got_ref)):
            for dy in range(HI * LO):
                for x in range(X):
                    row, lanes = dy * 4 + x // 2, slice(x % 2 * 64, x % 2 * 64 + 64)
                    out_ref[(y ^ dy) * X + x, model : model + 1, :] = jnp.concatenate(
                        [ref[row : row + 1, lanes], ref[row + 2 : row + 3, lanes]], axis=1
                    )

    @pl.when(core == 1)
    def _():
        for model, ref in enumerate((keep_ref, got_ref)):
            for planes in range(Z):
                row = planes // 2 * 4 + planes % 2
                to = lax.rem(z + Z - planes, Z)
                out_ref[to * HI + hi, model : model + 1, :] = ref[row : row + 1, :]


def last_kernel(place, mine_ref, got_ref, image_ref, text_ref):
    mine, got = jnp.sum(mine_ref[...], axis=0), jnp.sum(got_ref[...], axis=0)

    @pl.when(place[2] == 0)
    def _():
        image_ref[...] = mine[:, :64]
        text_ref[0:1, :] = got[1:2, :64]
        text_ref[1:2, :] = got[0:1, :64]

    @pl.when(place[2] == 1)
    def _():
        image_ref[...] = got[:, 64:]
        text_ref[0:1, :] = mine[1:2, 64:]
        text_ref[1:2, :] = mine[0:1, 64:]


def reduce_sums(place, keep, give):
    def part(*shape):
        return jax.ShapeDtypeStruct(shape, jnp.float32)

    def call(kernel, specs, outs, *operands):
        return pl.pallas_call(
            kernel,
            in_specs=specs,
            out_specs=[VMEM] * len(outs),
            out_shape=outs,
            compiler_params=SMALL,
        )(*operands)

    groups = groups_by(
        lambda hi, z, c, lo, x: (c, lo, x) if c else (c, z, 0),
        lambda hi, z, c, lo, x: (z, hi) if c else (hi, lo, x),
    )
    chunks = HI * LO * X
    (sums,) = call(
        spread_kernel, [SMEM, VMEM, VMEM], [part(chunks, 2, 128)], place, keep, send_core(give)
    )
    mine = exchange(sums, groups)
    got = send_core(mine)
    return call(last_kernel, [SMEM, VMEM, VMEM], [part(2, 64)] * 2, place, mine, got)


def on_device(
    student_picture_vectors,
    student_caption_vectors,
    teacher_picture_vectors,
    teacher_caption_vectors,
    sharpness_factors,
    offset_couple,
):
    features = student_picture_vectors.shape[0]
    narrow = lax.axis_index("narrow")
    wide = lax.axis_index("wide")
    core = wide % CORES
    place = jnp.stack([narrow, wide // (Z * CORES), core, wide // CORES % Z]).astype(jnp.int32)
    learner = core == 0

    own_pictures, pictures, shares = start(
        (student_picture_vectors, teacher_picture_vectors),
        (student_caption_vectors, teacher_caption_vectors),
    )

    by_row = groups_by(lambda hi, z, c, lo, x: (hi, z), lambda hi, z, c, lo, x: (c, lo, x))
    text = text_rows(place, exchange(shares, by_row), features)

    other_pictures = send_core(pictures)
    both = jnp.where(
        learner,
        jnp.stack([own_pictures, other_pictures]),
        jnp.stack([other_pictures, own_pictures]),
    )
    ring = [both] + [send_first(both, d) for d in (1, 2, 3)]
    _, *ring = lax.optimization_barrier((text, *ring))
    line = jnp.stack(ring)
    one, three = send_second(line, 1), send_second(line, 3)
    two_low, two_high = send_second(three[:2], 1), send_second(one[2:], 3)

    up1, down1 = send_z(text, 1), send_z(text, -1)
    up2, down2 = send_z(up1, 1), send_z(down1, -1)
    up3, down3 = send_z(up2, 1), send_z(down2, -1)
    down4 = send_z(down3, -1)

    scalars = (sharpness_factors, offset_couple, place)
    image_sums, text_sums, image, scale = pair_sums(
        *scalars, (text, up1, down1, up2, down2), (line, one, two_low, two_high, three), True
    )
    keep, give = pair_sums(
        *scalars, (up3, down3, down4), (image, scale, image_sums, text_sums), False
    )
    return tuple(reduce_sums(place, keep, give))


def solution(mesh):
    return jax.shard_map(
        on_device,
        mesh=mesh,
        in_specs=(
            P("narrow", "wide"),
            P("narrow", "wide"),
            P("narrow", "wide"),
            P("narrow", "wide"),
            P(),
            P(),
        ),
        out_specs=(P(None, ("wide", "narrow")), P(None, ("wide", "narrow"))),
        check_vma=False,
    )
```

```python
import functools

import jax
import jax.numpy as jnp
from jax import lax
from jax.experimental import pallas as pl
from jax.experimental.pallas import tpu as pltpu
from jax.sharding import PartitionSpec as P

epsilon = 1e-06
AXES = ("wide", "narrow")
X, LO, HI, Z, CORES = 4, 2, 2, 8, 2
NARROW = LO * X


def device(hi, z, core, lo, x):
    return ((hi * Z + z) * CORES + core) * NARROW + lo * X + x


def places():
    for hi in range(HI):
        for z in range(Z):
            for core in range(CORES):
                for lo in range(LO):
                    for x in range(X):
                        yield hi, z, core, lo, x


def send(value, step):
    pairs = [(place, step(*place)) for place in places()]
    pairs = [(device(*place), device(*target)) for place, target in pairs if target]
    return lax.ppermute(value, AXES, pairs)


def send_core(value):
    return send(value, lambda hi, z, core, lo, x: (hi, z, core ^ 1, lo, x))


def send_first(value, d):
    return send(
        value,
        lambda hi, z, core, lo, x: (
            (hi ^ (d >> 1), z, core, lo ^ (d & 1), x) if core else (hi, z, core, lo, x ^ d)
        ),
    )


def send_second(value, d):
    return send(
        value,
        lambda hi, z, core, lo, x: (
            (hi, z, core, lo, x ^ d) if core else (hi ^ (d >> 1), z, core, lo ^ (d & 1), x)
        ),
    )


def groups_by(key, order):
    groups = {}
    for place in places():
        groups.setdefault(key(*place), []).append(place)
    return [
        [device(*place) for place in sorted(group, key=lambda place: order(*place))]
        for group in groups.values()
    ]


def exchange(value, groups):
    return lax.all_to_all(value, AXES, 0, 0, axis_index_groups=groups, tiled=True)


def send_z(value, dz):
    return send(value, lambda hi, z, core, lo, x: (hi, (z + dz) % Z, core, lo, x))


VMEM = pl.BlockSpec(memory_space=pltpu.VMEM)
SMEM = pl.BlockSpec(memory_space=pltpu.SMEM)
LARGE = 60 * 1024 * 1024
SMALL = pltpu.CompilerParams(vmem_limit_bytes=4 * 1024 * 1024)


FOLD = 80


def shares_kernel(learner_ref, refer_ref, out_ref):
    features, block = learner_ref.shape
    share = block // NARROW
    for model, ref in enumerate((learner_ref, refer_ref)):
        for n in range(NARROW):
            piece = ref[:, n * share : (n + 1) * share]
            rest = jnp.concatenate(
                [piece[FOLD:], jnp.zeros((2 * FOLD - features, share), piece.dtype)], axis=0
            )
            out_ref[model * NARROW + n] = jnp.concatenate([piece[:FOLD], rest], axis=1)


def text_shares(learner, refer):
    _, block = learner.shape
    return pl.pallas_call(
        shares_kernel,
        in_specs=[VMEM, VMEM],
        out_specs=VMEM,
        out_shape=jax.ShapeDtypeStruct(
            (CORES * NARROW, FOLD, 2 * block // NARROW), learner.dtype
        ),
        compiler_params=pltpu.CompilerParams(vmem_limit_bytes=LARGE),
    )(learner, refer)


def rows_kernel(place, in_ref, out_ref):
    features = out_ref.shape[1] // NARROW
    share = out_ref.shape[0] // CORES
    columns = []
    for other in range(CORES):
        parts = []
        for slot in range(NARROW):
            piece = in_ref[(place[2] ^ other) * NARROW + (place[0] ^ slot)]
            parts += [piece[:, :share], piece[: features - FOLD, share:]]
        columns.append(jnp.concatenate(parts, axis=0))
    out_ref[...] = jnp.concatenate(columns, axis=1).T


def text_rows(place, shares, features):
    return pl.pallas_call(
        rows_kernel,
        in_specs=[SMEM, VMEM],
        out_specs=VMEM,
        out_shape=jax.ShapeDtypeStruct((shares.shape[2], NARROW * features), shares.dtype),
        compiler_params=SMALL,
    )(place, shares)


def tail_power(value):
    return jnp.exp2(jnp.abs(value) * -1.4426950408889634)


def both_tails(a, b):
    return (a + b) + a * b


def log_tail(tail):
    near = 1.0 + tail
    return jnp.log(near) + (tail - (near - 1.0))


def pair_kernel(sharpness, offsets, place, *refs, texts, first):
    text_refs, refs = refs[:texts], refs[texts:]
    text, even, odd, text_scale, total = refs[-5:]
    if first:
        line, one, two_low, two_high, three, image_sums, text_sums, image, image_scale = refs[:9]
    else:
        image, image_scale, before_image, before_text, keep_out, give_out = refs[:6]
        image_sums, text_sums = refs[6:8]
    narrow, hi, core = place[0], place[1], place[2]
    low = narrow // X
    temper = jnp.where(core == 0, sharpness[0], sharpness[1])
    offset = jnp.where(core == 0, offsets[0], offsets[1])
    rows, depth = text.shape
    columns = image.shape[4]

    row = 0
    for ref in text_refs:
        size = ref.shape[0]
        text[row : row + size, :] = ref[...]
        row += size

    if first:

        @pl.when(core == 0)
        def _():
            for block in range(4):
                owner = block // 2
                if block % 2 == 0:
                    image[block, 0] = line[:, owner]
                    image[block, 1] = one[:, owner]
                else:
                    image[block, 0, 0:2] = two_low[:, owner]
                    image[block, 0, 2:4] = two_high[:, owner]
                    image[block, 1] = three[:, owner]

        @pl.when(core == 1)
        def _():
            for block in range(4):
                owner, at = block // 2, slice(block % 2 * 2, block % 2 * 2 + 2)
                two = two_high if block % 2 else two_low
                image[block, :, 0] = line[at, owner]
                image[block, :, 1] = one[at, owner]
                image[block, :, 2] = two[:, owner]
                image[block, :, 3] = three[at, owner]

    total[...] = jnp.zeros_like(total)

    @pl.loop(0, rows // 128)
    def _(i):
        at = pl.ds(pl.multiple_of(i * 128, 128), 128)
        squares = jnp.square(text[at, :].astype(jnp.float32))
        norm = jnp.sum(squares, axis=1, keepdims=True) + epsilon
        text_scale[at, :] = jnp.broadcast_to(temper * lax.rsqrt(norm), (128, 128))

    def scale_block(block):
        flat = image.at[block].reshape(depth, columns)
        norm = jnp.zeros((8, columns), jnp.float32)
        for r in range(0, depth, 32):
            part = jnp.square(flat[r : r + 32, :].astype(jnp.float32))
            norm += jnp.sum(part.reshape(4, 8, columns), axis=0)
        norm = jnp.sum(norm, axis=0, keepdims=True) + epsilon
        image_scale[block] = lax.rsqrt(norm)

    span = even.shape[0]
    parts = rows // span

    def product(block, part, out):
        flat = image.at[block].reshape(depth, columns)
        out[...] = jnp.dot(
            text[part * span : (part + 1) * span, :],
            flat[...],
            preferred_element_type=jnp.float32,
        )

    def losses(block, part, products):
        owner, high = block // 2, block % 2
        across = image_scale[block]
        image_total = jnp.zeros((8, columns), jnp.float32)
        step = 32
        column_tail = None
        for r in range(0, span, step):
            at = slice(part * span + r, part * span + r + step)
            down = text_scale[at, :]
            down = jnp.concatenate([down] * (columns // 128), axis=1)
            logit = products[r : r + step, :] * down * across + offset
            if first and high == 0 and part == 0 and r < 128:
                mine = owner == (core ^ (r // 64))
                shift = jnp.where(mine, narrow * 64 + r % 64, -columns)
                i = lax.broadcasted_iota(jnp.int32, logit.shape, 0)
                j = lax.broadcasted_iota(jnp.int32, logit.shape, 1)
                logit = jnp.where(j - i == shift, -logit, logit)
            above = jnp.maximum(logit, 0.0)
            tail = tail_power(logit)
            tiles = [slice(lane, lane + 128) for lane in range(0, columns, 128)]
            row_tail = functools.reduce(both_tails, [tail[:, tile] for tile in tiles])
            total[at, :] += log_tail(row_tail) + sum(above[:, tile] for tile in tiles)
            for g in range(0, step, 8):
                group = tail[g : g + 8, :]
                column_tail = group if column_tail is None else both_tails(column_tail, group)
            image_total += jnp.sum(above.reshape(step // 8, 8, columns), axis=0)
            if r % 64 or r + step == span:
                image_total += log_tail(column_tail)
                column_tail = None
        summed = jnp.sum(image_total, axis=0, keepdims=True)
        for j in range(columns // 128):
            row = (high * 2 + ((j // 2) ^ low)) * 4 + owner * 2 + j % 2
            lanes = summed[:, j * 128 : (j + 1) * 128]
            if part == 0:
                image_sums[pl.ds(row, 1), :] = lanes
            else:
                image_sums[pl.ds(row, 1), :] += lanes

    steps = [(block, part) for block in range(4) for part in range(parts)]
    buffers = (even, odd)
    for n, step in enumerate(steps + [None]):
        if step is not None:
            if first and step[1] == 0:
                scale_block(step[0])
            product(*step, buffers[n % 2])
        if n > 0:
            losses(*steps[n - 1], buffers[(n - 1) % 2])

    text_sums[...] = jnp.zeros_like(text_sums) if first else before_text[...]
    for i, planes in enumerate((0, 1, 7, 2, 6) if first else (3, 5, 4)):
        summed = jnp.sum(total[i * 128 : (i + 1) * 128, :].T, axis=0, keepdims=True)
        summed = jnp.where(core == 0, summed, pltpu.roll(summed, 64, 1))
        row = planes // 2 * 4 + planes % 2
        text_sums[row : row + 1, :] = summed
    if not first:
        images_all = image_sums[...] + before_image[...]
        keep_out[...] = jnp.where(core == 0, images_all, text_sums[...])
        give_out[...] = jnp.where(core == 0, text_sums[...], images_all)


def pair_sums(sharpness, offsets, place, texts, operands, first):
    rows = sum(text.shape[0] for text in texts)
    depth = texts[0].shape[1]
    features, columns = operands[0].shape[-2:]
    sums = jax.ShapeDtypeStruct((16, 128), jnp.float32)
    outs = [sums, sums]
    span = rows // (2 if first else 3)
    buffers = [
        pltpu.VMEM((rows, depth), jnp.bfloat16),
        pltpu.VMEM((span, columns), jnp.float32),
        pltpu.VMEM((span, columns), jnp.float32),
        pltpu.VMEM((rows, 128), jnp.float32),
        pltpu.VMEM((rows, 128), jnp.float32),
    ]
    if first:
        outs += [
            jax.ShapeDtypeStruct((4, LO, X, features, columns), jnp.bfloat16),
            jax.ShapeDtypeStruct((4, 1, columns), jnp.float32),
        ]
    else:
        buffers = [pltpu.VMEM((16, 128), jnp.float32)] * 2 + buffers
    operands = (*texts, *operands)
    return pl.pallas_call(
        functools.partial(pair_kernel, texts=len(texts), first=first),
        in_specs=[SMEM] * 3 + [VMEM] * len(operands),
        out_specs=[VMEM] * len(outs),
        out_shape=outs,
        scratch_shapes=buffers,
        compiler_params=pltpu.CompilerParams(vmem_limit_bytes=24 * 1024 * 1024),
        cost_estimate=pl.CostEstimate(
            flops=8 * rows * columns * depth,
            bytes_accessed=2 * depth * (rows + 4 * columns),
            transcendentals=8 * rows * columns,
        ),
    )(sharpness, offsets, place, *operands)


def spread_kernel(place, keep_ref, got_ref, out_ref):
    narrow, hi, core, z = place[0], place[1], place[2], place[3]
    y = hi * 2 + narrow // X
    out_ref[...] = jnp.zeros_like(out_ref)

    @pl.when(core == 0)
    def _():
        for model, ref in enumerate((keep_ref, got_ref)):
            for dy in range(HI * LO):
                for x in range(X):
                    row, lanes = dy * 4 + x // 2, slice(x % 2 * 64, x % 2 * 64 + 64)
                    out_ref[(y ^ dy) * X + x, model : model + 1, :] = jnp.concatenate(
                        [ref[row : row + 1, lanes], ref[row + 2 : row + 3, lanes]], axis=1
                    )

    @pl.when(core == 1)
    def _():
        for model, ref in enumerate((keep_ref, got_ref)):
            for planes in range(Z):
                row = planes // 2 * 4 + planes % 2
                to = lax.rem(z + Z - planes, Z)
                out_ref[to * HI + hi, model : model + 1, :] = ref[row : row + 1, :]


def last_kernel(place, mine_ref, got_ref, image_ref, text_ref):
    mine, got = jnp.sum(mine_ref[...], axis=0), jnp.sum(got_ref[...], axis=0)

    @pl.when(place[2] == 0)
    def _():
        image_ref[...] = mine[:, :64]
        text_ref[0:1, :] = got[1:2, :64]
        text_ref[1:2, :] = got[0:1, :64]

    @pl.when(place[2] == 1)
    def _():
        image_ref[...] = got[:, 64:]
        text_ref[0:1, :] = mine[1:2, 64:]
        text_ref[1:2, :] = mine[0:1, 64:]


def reduce_sums(place, keep, give):
    def part(*shape):
        return jax.ShapeDtypeStruct(shape, jnp.float32)

    def call(kernel, specs, outs, *operands):
        return pl.pallas_call(
            kernel,
            in_specs=specs,
            out_specs=[VMEM] * len(outs),
            out_shape=outs,
            compiler_params=SMALL,
        )(*operands)

    groups = groups_by(
        lambda hi, z, c, lo, x: (c, lo, x) if c else (c, z, 0),
        lambda hi, z, c, lo, x: (z, hi) if c else (hi, lo, x),
    )
    chunks = HI * LO * X
    (sums,) = call(
        spread_kernel, [SMEM, VMEM, VMEM], [part(chunks, 2, 128)], place, keep, send_core(give)
    )
    mine = exchange(sums, groups)
    got = send_core(mine)
    return call(last_kernel, [SMEM, VMEM, VMEM], [part(2, 64)] * 2, place, mine, got)


def on_device(
    student_picture_vectors,
    student_caption_vectors,
    teacher_picture_vectors,
    teacher_caption_vectors,
    sharpness_factors,
    offset_couple,
):
    features = student_picture_vectors.shape[0]
    narrow = lax.axis_index("narrow")
    wide = lax.axis_index("wide")
    core = wide % CORES
    place = jnp.stack([narrow, wide // (Z * CORES), core, wide // CORES % Z]).astype(jnp.int32)
    learner = core == 0

    pictures = jnp.where(learner, teacher_picture_vectors, student_picture_vectors)
    other_pictures = send_core(pictures)
    shares = text_shares(student_caption_vectors, teacher_caption_vectors)
    both = jnp.where(
        learner,
        jnp.stack([student_picture_vectors, other_pictures]),
        jnp.stack([other_pictures, teacher_picture_vectors]),
    )
    both, shares = lax.optimization_barrier((both, shares))
    ring = [both] + [send_first(both, d) for d in (1, 2, 3)]

    by_row = groups_by(lambda hi, z, c, lo, x: (hi, z), lambda hi, z, c, lo, x: (c, lo, x))
    text = text_rows(place, exchange(shares, by_row), features)
    _, *ring = lax.optimization_barrier((text, *ring))
    line = jnp.stack(ring)
    one, three = send_second(line, 1), send_second(line, 3)
    two_low, two_high = send_second(three[:2], 1), send_second(one[2:], 3)

    up1, down1 = send_z(text, 1), send_z(text, -1)
    up2, down2 = send_z(up1, 1), send_z(down1, -1)
    up3, down3 = send_z(up2, 1), send_z(down2, -1)
    down4 = send_z(down3, -1)

    scalars = (sharpness_factors, offset_couple, place)
    image_sums, text_sums, image, scale = pair_sums(
        *scalars, (text, up1, down1, up2, down2), (line, one, two_low, two_high, three), True
    )
    keep, give = pair_sums(
        *scalars, (up3, down3, down4), (image, scale, image_sums, text_sums), False
    )
    return tuple(reduce_sums(place, keep, give))


def solution(mesh):
    return jax.shard_map(
        on_device,
        mesh=mesh,
        in_specs=(
            P("narrow", "wide"),
            P("narrow", "wide"),
            P("narrow", "wide"),
            P("narrow", "wide"),
            P(),
            P(),
        ),
        out_specs=(P(None, ("wide", "narrow")), P(None, ("wide", "narrow"))),
        check_vma=False,
    )
```

```python
import functools

import jax
import jax.numpy as jnp
from jax import lax
from jax.experimental import pallas as pl
from jax.experimental.pallas import tpu as pltpu
from jax.sharding import PartitionSpec as P

epsilon = 1e-06
AXES = ("wide", "narrow")
X, LO, HI, Z, CORES = 4, 2, 2, 8, 2
NARROW = LO * X


def device(hi, z, core, lo, x):
    return ((hi * Z + z) * CORES + core) * NARROW + lo * X + x


def places():
    for hi in range(HI):
        for z in range(Z):
            for core in range(CORES):
                for lo in range(LO):
                    for x in range(X):
                        yield hi, z, core, lo, x


def send(value, step):
    pairs = [(place, step(*place)) for place in places()]
    pairs = [(device(*place), device(*target)) for place, target in pairs if target]
    return lax.ppermute(value, AXES, pairs)


def send_core(value):
    return send(value, lambda hi, z, core, lo, x: (hi, z, core ^ 1, lo, x))


def send_first(value, d):
    return send(
        value,
        lambda hi, z, core, lo, x: (
            (hi ^ (d >> 1), z, core, lo ^ (d & 1), x) if core else (hi, z, core, lo, x ^ d)
        ),
    )


def send_second(value, d):
    return send(
        value,
        lambda hi, z, core, lo, x: (
            (hi, z, core, lo, x ^ d) if core else (hi ^ (d >> 1), z, core, lo ^ (d & 1), x)
        ),
    )


def groups_by(key, order):
    groups = {}
    for place in places():
        groups.setdefault(key(*place), []).append(place)
    return [
        [device(*place) for place in sorted(group, key=lambda place: order(*place))]
        for group in groups.values()
    ]


def exchange(value, groups):
    return lax.all_to_all(value, AXES, 0, 0, axis_index_groups=groups, tiled=True)


def send_z(value, dz):
    return send(value, lambda hi, z, core, lo, x: (hi, (z + dz) % Z, core, lo, x))


VMEM = pl.BlockSpec(memory_space=pltpu.VMEM)
SMEM = pl.BlockSpec(memory_space=pltpu.SMEM)
LARGE = 60 * 1024 * 1024
SMALL = pltpu.CompilerParams(vmem_limit_bytes=4 * 1024 * 1024)


FOLD = 80


def shares_kernel(learner_ref, refer_ref, out_ref):
    features, block = learner_ref.shape
    share = block // NARROW
    for model, ref in enumerate((learner_ref, refer_ref)):
        for n in range(NARROW):
            piece = ref[:, n * share : (n + 1) * share]
            rest = jnp.concatenate(
                [piece[FOLD:], jnp.zeros((2 * FOLD - features, share), piece.dtype)], axis=0
            )
            out_ref[model * NARROW + n] = jnp.concatenate([piece[:FOLD], rest], axis=1)


def text_shares(learner, refer):
    _, block = learner.shape
    return pl.pallas_call(
        shares_kernel,
        in_specs=[VMEM, VMEM],
        out_specs=VMEM,
        out_shape=jax.ShapeDtypeStruct(
            (CORES * NARROW, FOLD, 2 * block // NARROW), learner.dtype
        ),
        compiler_params=pltpu.CompilerParams(vmem_limit_bytes=LARGE),
    )(learner, refer)


def rows_kernel(place, in_ref, out_ref):
    features = out_ref.shape[1] // NARROW
    share = out_ref.shape[0] // CORES
    columns = []
    for other in range(CORES):
        parts = []
        for slot in range(NARROW):
            piece = in_ref[(place[2] ^ other) * NARROW + (place[0] ^ slot)]
            parts += [piece[:, :share], piece[: features - FOLD, share:]]
        columns.append(jnp.concatenate(parts, axis=0))
    out_ref[...] = jnp.concatenate(columns, axis=1).T


def text_rows(place, shares, features):
    return pl.pallas_call(
        rows_kernel,
        in_specs=[SMEM, VMEM],
        out_specs=VMEM,
        out_shape=jax.ShapeDtypeStruct((shares.shape[2], NARROW * features), shares.dtype),
        compiler_params=SMALL,
        cost_estimate=pl.CostEstimate(flops=0, bytes_accessed=4096, transcendentals=0),
    )(place, shares)


def tail_power(value):
    return jnp.exp2(jnp.abs(value) * -1.4426950408889634)


def both_tails(a, b):
    return (a + b) + a * b


def log_tail(tail):
    near = 1.0 + tail
    return jnp.log(near) + (tail - (near - 1.0))


def pair_kernel(sharpness, offsets, place, *refs, texts, first):
    text_refs, refs = refs[:texts], refs[texts:]
    text, even, odd, text_scale, total = refs[-5:]
    if first:
        line, one, two_low, two_high, three, image_sums, text_sums, image, image_scale = refs[:9]
    else:
        image, image_scale, before_image, before_text, keep_out, give_out = refs[:6]
        image_sums, text_sums = refs[6:8]
    narrow, hi, core = place[0], place[1], place[2]
    low = narrow // X
    temper = jnp.where(core == 0, sharpness[0], sharpness[1])
    offset = jnp.where(core == 0, offsets[0], offsets[1])
    rows, depth = text.shape
    columns = image.shape[4]

    row = 0
    for ref in text_refs:
        size = ref.shape[0]
        text[row : row + size, :] = ref[...]
        row += size

    if first:

        @pl.when(core == 0)
        def _():
            for block in range(4):
                owner = block // 2
                if block % 2 == 0:
                    image[block, 0] = line[:, owner]
                    image[block, 1] = one[:, owner]
                else:
                    image[block, 0, 0:2] = two_low[:, owner]
                    image[block, 0, 2:4] = two_high[:, owner]
                    image[block, 1] = three[:, owner]

        @pl.when(core == 1)
        def _():
            for block in range(4):
                owner, at = block // 2, slice(block % 2 * 2, block % 2 * 2 + 2)
                two = two_high if block % 2 else two_low
                image[block, :, 0] = line[at, owner]
                image[block, :, 1] = one[at, owner]
                image[block, :, 2] = two[:, owner]
                image[block, :, 3] = three[at, owner]

    total[...] = jnp.zeros_like(total)

    @pl.loop(0, rows // 128)
    def _(i):
        at = pl.ds(pl.multiple_of(i * 128, 128), 128)
        squares = jnp.square(text[at, :].astype(jnp.float32))
        norm = jnp.sum(squares, axis=1, keepdims=True) + epsilon
        text_scale[at, :] = jnp.broadcast_to(temper * lax.rsqrt(norm), (128, 128))

    def scale_block(block):
        flat = image.at[block].reshape(depth, columns)
        norm = jnp.zeros((8, columns), jnp.float32)
        for r in range(0, depth, 32):
            part = jnp.square(flat[r : r + 32, :].astype(jnp.float32))
            norm += jnp.sum(part.reshape(4, 8, columns), axis=0)
        norm = jnp.sum(norm, axis=0, keepdims=True) + epsilon
        image_scale[block] = lax.rsqrt(norm)

    span = even.shape[0]
    parts = rows // span

    def product(block, part, out):
        flat = image.at[block].reshape(depth, columns)
        out[...] = jnp.dot(
            text[part * span : (part + 1) * span, :],
            flat[...],
            preferred_element_type=jnp.float32,
        )

    def losses(block, part, products):
        owner, high = block // 2, block % 2
        across = image_scale[block]
        image_total = jnp.zeros((8, columns), jnp.float32)
        step = 32
        column_tail = None
        for r in range(0, span, step):
            at = slice(part * span + r, part * span + r + step)
            down = text_scale[at, :]
            down = jnp.concatenate([down] * (columns // 128), axis=1)
            logit = products[r : r + step, :] * down * across + offset
            if first and high == 0 and part == 0 and r < 128:
                mine = owner == (core ^ (r // 64))
                shift = jnp.where(mine, narrow * 64 + r % 64, -columns)
                i = lax.broadcasted_iota(jnp.int32, logit.shape, 0)
                j = lax.broadcasted_iota(jnp.int32, logit.shape, 1)
                logit = jnp.where(j - i == shift, -logit, logit)
            above = jnp.maximum(logit, 0.0)
            tail = tail_power(logit)
            tiles = [slice(lane, lane + 128) for lane in range(0, columns, 128)]
            row_tail = functools.reduce(both_tails, [tail[:, tile] for tile in tiles])
            total[at, :] += log_tail(row_tail) + sum(above[:, tile] for tile in tiles)
            for g in range(0, step, 8):
                group = tail[g : g + 8, :]
                column_tail = group if column_tail is None else both_tails(column_tail, group)
            image_total += jnp.sum(above.reshape(step // 8, 8, columns), axis=0)
            if r % 64 or r + step == span:
                image_total += log_tail(column_tail)
                column_tail = None
        summed = jnp.sum(image_total, axis=0, keepdims=True)
        for j in range(columns // 128):
            row = (high * 2 + ((j // 2) ^ low)) * 4 + owner * 2 + j % 2
            lanes = summed[:, j * 128 : (j + 1) * 128]
            if part == 0:
                image_sums[pl.ds(row, 1), :] = lanes
            else:
                image_sums[pl.ds(row, 1), :] += lanes

    steps = [(block, part) for block in range(4) for part in range(parts)]
    buffers = (even, odd)
    for n, step in enumerate(steps + [None]):
        if step is not None:
            if first and step[1] == 0:
                scale_block(step[0])
            product(*step, buffers[n % 2])
        if n > 0:
            losses(*steps[n - 1], buffers[(n - 1) % 2])

    text_sums[...] = jnp.zeros_like(text_sums) if first else before_text[...]
    for i, planes in enumerate((0, 1, 7, 2, 6) if first else (3, 5, 4)):
        summed = jnp.sum(total[i * 128 : (i + 1) * 128, :].T, axis=0, keepdims=True)
        summed = jnp.where(core == 0, summed, pltpu.roll(summed, 64, 1))
        row = planes // 2 * 4 + planes % 2
        text_sums[row : row + 1, :] = summed
    if not first:
        images_all = image_sums[...] + before_image[...]
        keep_out[...] = jnp.where(core == 0, images_all, text_sums[...])
        give_out[...] = jnp.where(core == 0, text_sums[...], images_all)


def pair_sums(sharpness, offsets, place, texts, operands, first):
    rows = sum(text.shape[0] for text in texts)
    depth = texts[0].shape[1]
    features, columns = operands[0].shape[-2:]
    sums = jax.ShapeDtypeStruct((16, 128), jnp.float32)
    outs = [sums, sums]
    span = rows // (2 if first else 3)
    buffers = [
        pltpu.VMEM((rows, depth), jnp.bfloat16),
        pltpu.VMEM((span, columns), jnp.float32),
        pltpu.VMEM((span, columns), jnp.float32),
        pltpu.VMEM((rows, 128), jnp.float32),
        pltpu.VMEM((rows, 128), jnp.float32),
    ]
    if first:
        outs += [
            jax.ShapeDtypeStruct((4, LO, X, features, columns), jnp.bfloat16),
            jax.ShapeDtypeStruct((4, 1, columns), jnp.float32),
        ]
    else:
        buffers = [pltpu.VMEM((16, 128), jnp.float32)] * 2 + buffers
    operands = (*texts, *operands)
    return pl.pallas_call(
        functools.partial(pair_kernel, texts=len(texts), first=first),
        in_specs=[SMEM] * 3 + [VMEM] * len(operands),
        out_specs=[VMEM] * len(outs),
        out_shape=outs,
        scratch_shapes=buffers,
        compiler_params=pltpu.CompilerParams(vmem_limit_bytes=24 * 1024 * 1024),
        cost_estimate=pl.CostEstimate(
            flops=8 * rows * columns * depth,
            bytes_accessed=2 * depth * (rows + 4 * columns),
            transcendentals=8 * rows * columns,
        ),
    )(sharpness, offsets, place, *operands)


def spread_kernel(place, keep_ref, got_ref, out_ref):
    narrow, hi, core, z = place[0], place[1], place[2], place[3]
    y = hi * 2 + narrow // X
    out_ref[...] = jnp.zeros_like(out_ref)

    @pl.when(core == 0)
    def _():
        for model, ref in enumerate((keep_ref, got_ref)):
            for dy in range(HI * LO):
                for x in range(X):
                    row, lanes = dy * 4 + x // 2, slice(x % 2 * 64, x % 2 * 64 + 64)
                    out_ref[(y ^ dy) * X + x, model : model + 1, :] = jnp.concatenate(
                        [ref[row : row + 1, lanes], ref[row + 2 : row + 3, lanes]], axis=1
                    )

    @pl.when(core == 1)
    def _():
        for model, ref in enumerate((keep_ref, got_ref)):
            for planes in range(Z):
                row = planes // 2 * 4 + planes % 2
                to = lax.rem(z + Z - planes, Z)
                out_ref[to * HI + hi, model : model + 1, :] = ref[row : row + 1, :]


def last_kernel(place, mine_ref, got_ref, image_ref, text_ref):
    mine, got = jnp.sum(mine_ref[...], axis=0), jnp.sum(got_ref[...], axis=0)

    @pl.when(place[2] == 0)
    def _():
        image_ref[...] = mine[:, :64]
        text_ref[0:1, :] = got[1:2, :64]
        text_ref[1:2, :] = got[0:1, :64]

    @pl.when(place[2] == 1)
    def _():
        image_ref[...] = got[:, 64:]
        text_ref[0:1, :] = mine[1:2, 64:]
        text_ref[1:2, :] = mine[0:1, 64:]


def reduce_sums(place, keep, give):
    def part(*shape):
        return jax.ShapeDtypeStruct(shape, jnp.float32)

    def call(kernel, specs, outs, *operands):
        return pl.pallas_call(
            kernel,
            in_specs=specs,
            out_specs=[VMEM] * len(outs),
            out_shape=outs,
            compiler_params=SMALL,
        )(*operands)

    groups = groups_by(
        lambda hi, z, c, lo, x: (c, lo, x) if c else (c, z, 0),
        lambda hi, z, c, lo, x: (z, hi) if c else (hi, lo, x),
    )
    chunks = HI * LO * X
    (sums,) = call(
        spread_kernel, [SMEM, VMEM, VMEM], [part(chunks, 2, 128)], place, keep, send_core(give)
    )
    mine = exchange(sums, groups)
    got = send_core(mine)
    return call(last_kernel, [SMEM, VMEM, VMEM], [part(2, 64)] * 2, place, mine, got)


def on_device(
    student_picture_vectors,
    student_caption_vectors,
    teacher_picture_vectors,
    teacher_caption_vectors,
    sharpness_factors,
    offset_couple,
):
    features = student_picture_vectors.shape[0]
    narrow = lax.axis_index("narrow")
    wide = lax.axis_index("wide")
    core = wide % CORES
    place = jnp.stack([narrow, wide // (Z * CORES), core, wide // CORES % Z]).astype(jnp.int32)
    learner = core == 0

    pictures = jnp.where(learner, teacher_picture_vectors, student_picture_vectors)
    other_pictures = send_core(pictures)
    shares = text_shares(student_caption_vectors, teacher_caption_vectors)
    both = jnp.where(
        learner,
        jnp.stack([student_picture_vectors, other_pictures]),
        jnp.stack([other_pictures, teacher_picture_vectors]),
    )
    both, shares = lax.optimization_barrier((both, shares))
    ring = [both] + [send_first(both, d) for d in (1, 2, 3)]

    by_row = groups_by(lambda hi, z, c, lo, x: (hi, z), lambda hi, z, c, lo, x: (c, lo, x))
    text = text_rows(place, exchange(shares, by_row), features)
    _, *ring = lax.optimization_barrier((text, *ring))
    line = jnp.stack(ring)
    one, three = send_second(line, 1), send_second(line, 3)
    two_low, two_high = send_second(three[:2], 1), send_second(one[2:], 3)

    up1, down1 = send_z(text, 1), send_z(text, -1)
    up2, down2 = send_z(up1, 1), send_z(down1, -1)
    up3, down3 = send_z(up2, 1), send_z(down2, -1)
    down4 = send_z(down3, -1)

    scalars = (sharpness_factors, offset_couple, place)
    image_sums, text_sums, image, scale = pair_sums(
        *scalars, (text, up1, down1, up2, down2), (line, one, two_low, two_high, three), True
    )
    keep, give = pair_sums(
        *scalars, (up3, down3, down4), (image, scale, image_sums, text_sums), False
    )
    return tuple(reduce_sums(place, keep, give))


def solution(mesh):
    return jax.shard_map(
        on_device,
        mesh=mesh,
        in_specs=(
            P("narrow", "wide"),
            P("narrow", "wide"),
            P("narrow", "wide"),
            P("narrow", "wide"),
            P(),
            P(),
        ),
        out_specs=(P(None, ("wide", "narrow")), P(None, ("wide", "narrow"))),
        check_vma=False,
    )
```

```python
import functools

import jax
import jax.numpy as jnp
from jax import lax
from jax.experimental import pallas as pl
from jax.experimental.pallas import tpu as pltpu
from jax.sharding import PartitionSpec as P

epsilon = 1e-06
AXES = ("wide", "narrow")
X, LO, HI, Z, CORES = 4, 2, 2, 8, 2
NARROW = LO * X


def device(hi, z, core, lo, x):
    return ((hi * Z + z) * CORES + core) * NARROW + lo * X + x


def places():
    for hi in range(HI):
        for z in range(Z):
            for core in range(CORES):
                for lo in range(LO):
                    for x in range(X):
                        yield hi, z, core, lo, x


def send(value, step):
    pairs = [(place, step(*place)) for place in places()]
    pairs = [(device(*place), device(*target)) for place, target in pairs if target]
    return lax.ppermute(value, AXES, pairs)


def send_core(value):
    return send(value, lambda hi, z, core, lo, x: (hi, z, core ^ 1, lo, x))


def send_first(value, d):
    return send(
        value,
        lambda hi, z, core, lo, x: (
            (hi ^ (d >> 1), z, core, lo ^ (d & 1), x) if core else (hi, z, core, lo, x ^ d)
        ),
    )


def send_second(value, d):
    return send(
        value,
        lambda hi, z, core, lo, x: (
            (hi, z, core, lo, x ^ d) if core else (hi ^ (d >> 1), z, core, lo ^ (d & 1), x)
        ),
    )


def groups_by(key, order):
    groups = {}
    for place in places():
        groups.setdefault(key(*place), []).append(place)
    return [
        [device(*place) for place in sorted(group, key=lambda place: order(*place))]
        for group in groups.values()
    ]


def exchange(value, groups):
    return lax.all_to_all(value, AXES, 0, 0, axis_index_groups=groups, tiled=True)


def send_z(value, dz):
    return send(value, lambda hi, z, core, lo, x: (hi, (z + dz) % Z, core, lo, x))


VMEM = pl.BlockSpec(memory_space=pltpu.VMEM)
SMEM = pl.BlockSpec(memory_space=pltpu.SMEM)
LARGE = 60 * 1024 * 1024
SMALL = pltpu.CompilerParams(vmem_limit_bytes=4 * 1024 * 1024)


FOLD = 80


def shares_kernel(learner_ref, refer_ref, out_ref):
    features, block = learner_ref.shape
    share = block // NARROW
    for model, ref in enumerate((learner_ref, refer_ref)):
        for n in range(NARROW):
            piece = ref[:, n * share : (n + 1) * share]
            rest = jnp.concatenate(
                [piece[FOLD:], jnp.zeros((2 * FOLD - features, share), piece.dtype)], axis=0
            )
            out_ref[model * NARROW + n] = jnp.concatenate([piece[:FOLD], rest], axis=1)


def text_shares(learner, refer):
    _, block = learner.shape
    return pl.pallas_call(
        shares_kernel,
        in_specs=[VMEM, VMEM],
        out_specs=VMEM,
        out_shape=jax.ShapeDtypeStruct(
            (CORES * NARROW, FOLD, 2 * block // NARROW), learner.dtype
        ),
        compiler_params=pltpu.CompilerParams(vmem_limit_bytes=LARGE),
    )(learner, refer)


def rows_kernel(place, in_ref, out_ref):
    features = out_ref.shape[1] // NARROW
    share = out_ref.shape[0] // CORES
    columns = []
    for other in range(CORES):
        parts = []
        for slot in range(NARROW):
            piece = in_ref[(place[2] ^ other) * NARROW + (place[0] ^ slot)]
            parts += [piece[:, :share], piece[: features - FOLD, share:]]
        columns.append(jnp.concatenate(parts, axis=0))
    out_ref[...] = jnp.concatenate(columns, axis=1).T


def text_rows(place, shares, features):
    return pl.pallas_call(
        rows_kernel,
        in_specs=[SMEM, VMEM],
        out_specs=VMEM,
        out_shape=jax.ShapeDtypeStruct((shares.shape[2], NARROW * features), shares.dtype),
        compiler_params=SMALL,
        cost_estimate=pl.CostEstimate(flops=0, bytes_accessed=4096, transcendentals=0),
    )(place, shares)


def tail_power(value):
    return jnp.exp2(jnp.abs(value) * -1.4426950408889634)


def both_tails(a, b):
    return (a + b) + a * b


def log_tail(tail):
    near = 1.0 + tail
    return jnp.log(near) + (tail - (near - 1.0))


def pair_kernel(sharpness, offsets, place, *refs, texts, first):
    text_refs, refs = refs[:texts], refs[texts:]
    text, even, odd, text_scale, total = refs[-5:]
    if first:
        line, one, two_low, two_high, three, image_sums, text_sums, image, image_scale = refs[:9]
    else:
        image, image_scale, before_image, before_text, keep_out, give_out = refs[:6]
        image_sums, text_sums = refs[6:8]
    narrow, hi, core = place[0], place[1], place[2]
    low = narrow // X
    temper = jnp.where(core == 0, sharpness[0], sharpness[1])
    offset = jnp.where(core == 0, offsets[0], offsets[1])
    rows, depth = text.shape
    columns = image.shape[4]

    row = 0
    for ref in text_refs:
        size = ref.shape[0]
        text[row : row + size, :] = ref[...]
        row += size

    if first:

        @pl.when(core == 0)
        def _():
            for block in range(4):
                owner = block // 2
                if block % 2 == 0:
                    image[block, 0] = line[:, owner]
                    image[block, 1] = one[:, owner]
                else:
                    image[block, 0, 0:2] = two_low[:, owner]
                    image[block, 0, 2:4] = two_high[:, owner]
                    image[block, 1] = three[:, owner]

        @pl.when(core == 1)
        def _():
            for block in range(4):
                owner, at = block // 2, slice(block % 2 * 2, block % 2 * 2 + 2)
                two = two_high if block % 2 else two_low
                image[block, :, 0] = line[at, owner]
                image[block, :, 1] = one[at, owner]
                image[block, :, 2] = two[:, owner]
                image[block, :, 3] = three[at, owner]

    total[...] = jnp.zeros_like(total)

    @pl.loop(0, rows // 128)
    def _(i):
        at = pl.ds(pl.multiple_of(i * 128, 128), 128)
        squares = jnp.square(text[at, :].astype(jnp.float32))
        norm = jnp.sum(squares, axis=1, keepdims=True) + epsilon
        text_scale[at, :] = jnp.broadcast_to(temper * lax.rsqrt(norm), (128, 128))

    def scale_block(block):
        flat = image.at[block].reshape(depth, columns)
        norm = jnp.zeros((8, columns), jnp.float32)
        for r in range(0, depth, 32):
            part = jnp.square(flat[r : r + 32, :].astype(jnp.float32))
            norm += jnp.sum(part.reshape(4, 8, columns), axis=0)
        norm = jnp.sum(norm, axis=0, keepdims=True) + epsilon
        image_scale[block] = lax.rsqrt(norm)

    span = even.shape[0]
    parts = rows // span

    def product(block, part, out):
        flat = image.at[block].reshape(depth, columns)
        rows_at = slice(part * span, (part + 1) * span)
        whole = depth // 256 * 256
        out[...] = jnp.dot(
            text[rows_at, :whole], flat[:whole, :], preferred_element_type=jnp.float32
        ) + jnp.dot(text[rows_at, whole:], flat[whole:, :], preferred_element_type=jnp.float32)

    def losses(block, part, products):
        owner, high = block // 2, block % 2
        across = image_scale[block]
        image_total = jnp.zeros((8, columns), jnp.float32)
        step = 32
        column_tail = None
        for r in range(0, span, step):
            at = slice(part * span + r, part * span + r + step)
            down = text_scale[at, :]
            down = jnp.concatenate([down] * (columns // 128), axis=1)
            logit = products[r : r + step, :] * down * across + offset
            if first and high == 0 and part == 0 and r < 128:
                mine = owner == (core ^ (r // 64))
                shift = jnp.where(mine, narrow * 64 + r % 64, -columns)
                i = lax.broadcasted_iota(jnp.int32, logit.shape, 0)
                j = lax.broadcasted_iota(jnp.int32, logit.shape, 1)
                logit = jnp.where(j - i == shift, -logit, logit)
            above = jnp.maximum(logit, 0.0)
            tail = tail_power(logit)
            tiles = [slice(lane, lane + 128) for lane in range(0, columns, 128)]
            row_tail = functools.reduce(both_tails, [tail[:, tile] for tile in tiles])
            total[at, :] += log_tail(row_tail) + sum(above[:, tile] for tile in tiles)
            for g in range(0, step, 8):
                group = tail[g : g + 8, :]
                column_tail = group if column_tail is None else both_tails(column_tail, group)
            image_total += jnp.sum(above.reshape(step // 8, 8, columns), axis=0)
            if r % 64 or r + step == span:
                image_total += log_tail(column_tail)
                column_tail = None
        summed = jnp.sum(image_total, axis=0, keepdims=True)
        for j in range(columns // 128):
            row = (high * 2 + ((j // 2) ^ low)) * 4 + owner * 2 + j % 2
            lanes = summed[:, j * 128 : (j + 1) * 128]
            if part == 0:
                image_sums[pl.ds(row, 1), :] = lanes
            else:
                image_sums[pl.ds(row, 1), :] += lanes

    steps = [(block, part) for block in range(4) for part in range(parts)]
    buffers = (even, odd)
    for n, step in enumerate(steps + [None]):
        if step is not None:
            if first and step[1] == 0:
                scale_block(step[0])
            product(*step, buffers[n % 2])
        if n > 0:
            losses(*steps[n - 1], buffers[(n - 1) % 2])

    text_sums[...] = jnp.zeros_like(text_sums) if first else before_text[...]
    for i, planes in enumerate((0, 1, 7, 2, 6) if first else (3, 5, 4)):
        summed = jnp.sum(total[i * 128 : (i + 1) * 128, :].T, axis=0, keepdims=True)
        summed = jnp.where(core == 0, summed, pltpu.roll(summed, 64, 1))
        row = planes // 2 * 4 + planes % 2
        text_sums[row : row + 1, :] = summed
    if not first:
        images_all = image_sums[...] + before_image[...]
        keep_out[...] = jnp.where(core == 0, images_all, text_sums[...])
        give_out[...] = jnp.where(core == 0, text_sums[...], images_all)


def pair_sums(sharpness, offsets, place, texts, operands, first):
    rows = sum(text.shape[0] for text in texts)
    depth = texts[0].shape[1]
    features, columns = operands[0].shape[-2:]
    sums = jax.ShapeDtypeStruct((16, 128), jnp.float32)
    outs = [sums, sums]
    span = rows // (2 if first else 3)
    buffers = [
        pltpu.VMEM((rows, depth), jnp.bfloat16),
        pltpu.VMEM((span, columns), jnp.float32),
        pltpu.VMEM((span, columns), jnp.float32),
        pltpu.VMEM((rows, 128), jnp.float32),
        pltpu.VMEM((rows, 128), jnp.float32),
    ]
    if first:
        outs += [
            jax.ShapeDtypeStruct((4, LO, X, features, columns), jnp.bfloat16),
            jax.ShapeDtypeStruct((4, 1, columns), jnp.float32),
        ]
    else:
        buffers = [pltpu.VMEM((16, 128), jnp.float32)] * 2 + buffers
    operands = (*texts, *operands)
    return pl.pallas_call(
        functools.partial(pair_kernel, texts=len(texts), first=first),
        in_specs=[SMEM] * 3 + [VMEM] * len(operands),
        out_specs=[VMEM] * len(outs),
        out_shape=outs,
        scratch_shapes=buffers,
        compiler_params=pltpu.CompilerParams(vmem_limit_bytes=24 * 1024 * 1024),
        cost_estimate=pl.CostEstimate(
            flops=8 * rows * columns * depth,
            bytes_accessed=2 * depth * (rows + 4 * columns),
            transcendentals=8 * rows * columns,
        ),
    )(sharpness, offsets, place, *operands)


def spread_kernel(place, keep_ref, got_ref, out_ref):
    narrow, hi, core, z = place[0], place[1], place[2], place[3]
    y = hi * 2 + narrow // X
    out_ref[...] = jnp.zeros_like(out_ref)

    @pl.when(core == 0)
    def _():
        for model, ref in enumerate((keep_ref, got_ref)):
            for dy in range(HI * LO):
                for x in range(X):
                    row, lanes = dy * 4 + x // 2, slice(x % 2 * 64, x % 2 * 64 + 64)
                    out_ref[(y ^ dy) * X + x, model : model + 1, :] = jnp.concatenate(
                        [ref[row : row + 1, lanes], ref[row + 2 : row + 3, lanes]], axis=1
                    )

    @pl.when(core == 1)
    def _():
        for model, ref in enumerate((keep_ref, got_ref)):
            for planes in range(Z):
                row = planes // 2 * 4 + planes % 2
                to = lax.rem(z + Z - planes, Z)
                out_ref[to * HI + hi, model : model + 1, :] = ref[row : row + 1, :]


def last_kernel(place, mine_ref, got_ref, image_ref, text_ref):
    mine, got = jnp.sum(mine_ref[...], axis=0), jnp.sum(got_ref[...], axis=0)

    @pl.when(place[2] == 0)
    def _():
        image_ref[...] = mine[:, :64]
        text_ref[0:1, :] = got[1:2, :64]
        text_ref[1:2, :] = got[0:1, :64]

    @pl.when(place[2] == 1)
    def _():
        image_ref[...] = got[:, 64:]
        text_ref[0:1, :] = mine[1:2, 64:]
        text_ref[1:2, :] = mine[0:1, 64:]


def reduce_sums(place, keep, give):
    def part(*shape):
        return jax.ShapeDtypeStruct(shape, jnp.float32)

    def call(kernel, specs, outs, *operands):
        return pl.pallas_call(
            kernel,
            in_specs=specs,
            out_specs=[VMEM] * len(outs),
            out_shape=outs,
            compiler_params=SMALL,
        )(*operands)

    groups = groups_by(
        lambda hi, z, c, lo, x: (c, lo, x) if c else (c, z, 0),
        lambda hi, z, c, lo, x: (z, hi) if c else (hi, lo, x),
    )
    chunks = HI * LO * X
    (sums,) = call(
        spread_kernel, [SMEM, VMEM, VMEM], [part(chunks, 2, 128)], place, keep, send_core(give)
    )
    mine = exchange(sums, groups)
    got = send_core(mine)
    return call(last_kernel, [SMEM, VMEM, VMEM], [part(2, 64)] * 2, place, mine, got)


def on_device(
    student_picture_vectors,
    student_caption_vectors,
    teacher_picture_vectors,
    teacher_caption_vectors,
    sharpness_factors,
    offset_couple,
):
    features = student_picture_vectors.shape[0]
    narrow = lax.axis_index("narrow")
    wide = lax.axis_index("wide")
    core = wide % CORES
    place = jnp.stack([narrow, wide // (Z * CORES), core, wide // CORES % Z]).astype(jnp.int32)
    learner = core == 0

    pictures = jnp.where(learner, teacher_picture_vectors, student_picture_vectors)
    other_pictures = send_core(pictures)
    shares = text_shares(student_caption_vectors, teacher_caption_vectors)
    both = jnp.where(
        learner,
        jnp.stack([student_picture_vectors, other_pictures]),
        jnp.stack([other_pictures, teacher_picture_vectors]),
    )
    both, shares = lax.optimization_barrier((both, shares))
    ring = [both] + [send_first(both, d) for d in (1, 2, 3)]

    by_row = groups_by(lambda hi, z, c, lo, x: (hi, z), lambda hi, z, c, lo, x: (c, lo, x))
    text = text_rows(place, exchange(shares, by_row), features)
    _, *ring = lax.optimization_barrier((text, *ring))
    line = jnp.stack(ring)
    one, three = send_second(line, 1), send_second(line, 3)
    two_low, two_high = send_second(three[:2], 1), send_second(one[2:], 3)

    up1, down1 = send_z(text, 1), send_z(text, -1)
    up2, down2 = send_z(up1, 1), send_z(down1, -1)
    up3, down3 = send_z(up2, 1), send_z(down2, -1)
    down4 = send_z(down3, -1)

    scalars = (sharpness_factors, offset_couple, place)
    image_sums, text_sums, image, scale = pair_sums(
        *scalars, (text, up1, down1, up2, down2), (line, one, two_low, two_high, three), True
    )
    keep, give = pair_sums(
        *scalars, (up3, down3, down4), (image, scale, image_sums, text_sums), False
    )
    return tuple(reduce_sums(place, keep, give))


def solution(mesh):
    return jax.shard_map(
        on_device,
        mesh=mesh,
        in_specs=(
            P("narrow", "wide"),
            P("narrow", "wide"),
            P("narrow", "wide"),
            P("narrow", "wide"),
            P(),
            P(),
        ),
        out_specs=(P(None, ("wide", "narrow")), P(None, ("wide", "narrow"))),
        check_vma=False,
    )
```

```python
import functools

import jax
import jax.numpy as jnp
from jax import lax
from jax.experimental import pallas as pl
from jax.experimental.pallas import tpu as pltpu
from jax.sharding import PartitionSpec as P

epsilon = 1e-06
AXES = ("wide", "narrow")
X, LO, HI, Z, CORES = 4, 2, 2, 8, 2
NARROW = LO * X


def device(hi, z, core, lo, x):
    return ((hi * Z + z) * CORES + core) * NARROW + lo * X + x


def places():
    for hi in range(HI):
        for z in range(Z):
            for core in range(CORES):
                for lo in range(LO):
                    for x in range(X):
                        yield hi, z, core, lo, x


def send(value, step):
    pairs = [(place, step(*place)) for place in places()]
    pairs = [(device(*place), device(*target)) for place, target in pairs if target]
    return lax.ppermute(value, AXES, pairs)


def send_core(value):
    return send(value, lambda hi, z, core, lo, x: (hi, z, core ^ 1, lo, x))


def send_first(value, d):
    return send(
        value,
        lambda hi, z, core, lo, x: (
            (hi ^ (d >> 1), z, core, lo ^ (d & 1), x) if core else (hi, z, core, lo, x ^ d)
        ),
    )


def send_second(value, d):
    return send(
        value,
        lambda hi, z, core, lo, x: (
            (hi, z, core, lo, x ^ d) if core else (hi ^ (d >> 1), z, core, lo ^ (d & 1), x)
        ),
    )


def groups_by(key, order):
    groups = {}
    for place in places():
        groups.setdefault(key(*place), []).append(place)
    return [
        [device(*place) for place in sorted(group, key=lambda place: order(*place))]
        for group in groups.values()
    ]


def exchange(value, groups):
    return lax.all_to_all(value, AXES, 0, 0, axis_index_groups=groups, tiled=True)


def send_z(value, dz):
    return send(value, lambda hi, z, core, lo, x: (hi, (z + dz) % Z, core, lo, x))


VMEM = pl.BlockSpec(memory_space=pltpu.VMEM)
SMEM = pl.BlockSpec(memory_space=pltpu.SMEM)
LARGE = 60 * 1024 * 1024
SMALL = pltpu.CompilerParams(vmem_limit_bytes=4 * 1024 * 1024)


FOLD = 80


def shares_kernel(learner_ref, refer_ref, out_ref):
    features, block = learner_ref.shape
    share = block // NARROW
    for model, ref in enumerate((learner_ref, refer_ref)):
        for n in range(NARROW):
            piece = ref[:, n * share : (n + 1) * share]
            rest = jnp.concatenate(
                [piece[FOLD:], jnp.zeros((2 * FOLD - features, share), piece.dtype)], axis=0
            )
            out_ref[model * NARROW + n] = jnp.concatenate([piece[:FOLD], rest], axis=1)


def text_shares(learner, refer):
    _, block = learner.shape
    return pl.pallas_call(
        shares_kernel,
        in_specs=[VMEM, VMEM],
        out_specs=VMEM,
        out_shape=jax.ShapeDtypeStruct(
            (CORES * NARROW, FOLD, 2 * block // NARROW), learner.dtype
        ),
        compiler_params=pltpu.CompilerParams(vmem_limit_bytes=LARGE),
    )(learner, refer)


def rows_kernel(place, in_ref, out_ref):
    features = out_ref.shape[1] // NARROW
    share = out_ref.shape[0] // CORES
    columns = []
    for other in range(CORES):
        parts = []
        for slot in range(NARROW):
            piece = in_ref[(place[2] ^ other) * NARROW + (place[0] ^ slot)]
            parts += [piece[:, :share], piece[: features - FOLD, share:]]
        columns.append(jnp.concatenate(parts, axis=0))
    out_ref[...] = jnp.concatenate(columns, axis=1).T


def text_rows(place, shares, features):
    return pl.pallas_call(
        rows_kernel,
        in_specs=[SMEM, VMEM],
        out_specs=VMEM,
        out_shape=jax.ShapeDtypeStruct((shares.shape[2], NARROW * features), shares.dtype),
        compiler_params=SMALL,
        cost_estimate=pl.CostEstimate(flops=0, bytes_accessed=4096, transcendentals=0),
    )(place, shares)


def tail_power(value):
    return jnp.exp2(jnp.abs(value) * -1.4426950408889634)


def both_tails(a, b):
    return (a + b) + a * b


def log_tail(tail):
    near = 1.0 + tail
    return jnp.log(near) + (tail - (near - 1.0))


def pair_kernel(sharpness, offsets, place, *refs, texts, first):
    text_refs, refs = refs[:texts], refs[texts:]
    text, even, odd, text_scale, total = refs[-5:]
    if first:
        line, one, two_low, two_high, three, image_sums, text_sums, image, image_scale = refs[:9]
    else:
        image, image_scale, before_image, before_text, keep_out, give_out = refs[:6]
        image_sums, text_sums = refs[6:8]
    narrow, hi, core = place[0], place[1], place[2]
    low = narrow // X
    temper = jnp.where(core == 0, sharpness[0], sharpness[1])
    offset = jnp.where(core == 0, offsets[0], offsets[1])
    rows, depth = text.shape
    columns = image.shape[4]

    row = 0
    for ref in text_refs:
        size = ref.shape[0]
        text[row : row + size, :] = ref[...]
        row += size

    if first:

        @pl.when(core == 0)
        def _():
            for block in range(4):
                owner = block // 2
                if block % 2 == 0:
                    image[block, 0] = line[:, owner]
                    image[block, 1] = one[:, owner]
                else:
                    image[block, 0, 0:2] = two_low[:, owner]
                    image[block, 0, 2:4] = two_high[:, owner]
                    image[block, 1] = three[:, owner]

        @pl.when(core == 1)
        def _():
            for block in range(4):
                owner, at = block // 2, slice(block % 2 * 2, block % 2 * 2 + 2)
                two = two_high if block % 2 else two_low
                image[block, :, 0] = line[at, owner]
                image[block, :, 1] = one[at, owner]
                image[block, :, 2] = two[:, owner]
                image[block, :, 3] = three[at, owner]

    total[...] = jnp.zeros_like(total)

    @pl.loop(0, rows // 128)
    def _(i):
        at = pl.ds(pl.multiple_of(i * 128, 128), 128)
        squares = jnp.square(text[at, :].astype(jnp.float32))
        norm = jnp.sum(squares, axis=1, keepdims=True) + epsilon
        text_scale[at, :] = jnp.broadcast_to(temper * lax.rsqrt(norm), (128, 128))

    def scale_block(block):
        flat = image.at[block].reshape(depth, columns)
        norm = jnp.zeros((8, columns), jnp.float32)
        for r in range(0, depth, 32):
            part = jnp.square(flat[r : r + 32, :].astype(jnp.float32))
            norm += jnp.sum(part.reshape(4, 8, columns), axis=0)
        norm = jnp.sum(norm, axis=0, keepdims=True) + epsilon
        image_scale[block] = lax.rsqrt(norm)

    span = even.shape[0]
    parts = rows // span

    def product(block, part, out):
        flat = image.at[block].reshape(depth, columns)
        rows_at = slice(part * span, (part + 1) * span)
        whole = depth // 256 * 256
        out[...] = jnp.dot(
            text[rows_at, :whole], flat[:whole, :], preferred_element_type=jnp.float32
        ) + jnp.dot(text[rows_at, whole:], flat[whole:, :], preferred_element_type=jnp.float32)

    def losses(block, part, products):
        owner, high = block // 2, block % 2
        across = image_scale[block]
        image_total = jnp.zeros((8, columns), jnp.float32)
        step = 32
        column_tail = None
        for r in range(0, span, step):
            at = slice(part * span + r, part * span + r + step)
            down = text_scale[at, :]
            down = jnp.concatenate([down] * (columns // 128), axis=1)
            logit = products[r : r + step, :] * down * across + offset
            if first and high == 0 and part == 0 and r < 128:
                mine = owner == (core ^ (r // 64))
                shift = jnp.where(mine, narrow * 64 + r % 64, -columns)
                i = lax.broadcasted_iota(jnp.int32, logit.shape, 0)
                j = lax.broadcasted_iota(jnp.int32, logit.shape, 1)
                logit = jnp.where(j - i == shift, -logit, logit)
            above = jnp.maximum(logit, 0.0)
            tail = tail_power(logit)
            tiles = [slice(lane, lane + 128) for lane in range(0, columns, 128)]
            row_tail = functools.reduce(both_tails, [tail[:, tile] for tile in tiles])
            total[at, :] += log_tail(row_tail) + sum(above[:, tile] for tile in tiles)
            for g in range(0, step, 8):
                group = tail[g : g + 8, :]
                column_tail = group if column_tail is None else both_tails(column_tail, group)
            image_total += jnp.sum(above.reshape(step // 8, 8, columns), axis=0)
            if r % 64 or r + step == span:
                image_total += log_tail(column_tail)
                column_tail = None
        summed = jnp.sum(image_total, axis=0, keepdims=True)
        for j in range(columns // 128):
            row = (high * 2 + ((j // 2) ^ low)) * 4 + owner * 2 + j % 2
            lanes = summed[:, j * 128 : (j + 1) * 128]
            if part == 0:
                image_sums[pl.ds(row, 1), :] = lanes
            else:
                image_sums[pl.ds(row, 1), :] += lanes

    steps = [(block, part) for block in range(4) for part in range(parts)]
    buffers = (even, odd)
    for n, step in enumerate(steps + [None]):
        if n > 0:
            losses(*steps[n - 1], buffers[(n - 1) % 2])
        if step is not None:
            if first and step[1] == 0:
                scale_block(step[0])
            product(*step, buffers[n % 2])

    text_sums[...] = jnp.zeros_like(text_sums) if first else before_text[...]
    for i, planes in enumerate((0, 1, 7, 2, 6) if first else (3, 5, 4)):
        summed = jnp.sum(total[i * 128 : (i + 1) * 128, :].T, axis=0, keepdims=True)
        summed = jnp.where(core == 0, summed, pltpu.roll(summed, 64, 1))
        row = planes // 2 * 4 + planes % 2
        text_sums[row : row + 1, :] = summed
    if not first:
        images_all = image_sums[...] + before_image[...]
        keep_out[...] = jnp.where(core == 0, images_all, text_sums[...])
        give_out[...] = jnp.where(core == 0, text_sums[...], images_all)


def pair_sums(sharpness, offsets, place, texts, operands, first):
    rows = sum(text.shape[0] for text in texts)
    depth = texts[0].shape[1]
    features, columns = operands[0].shape[-2:]
    sums = jax.ShapeDtypeStruct((16, 128), jnp.float32)
    outs = [sums, sums]
    span = rows // (2 if first else 3)
    buffers = [
        pltpu.VMEM((rows, depth), jnp.bfloat16),
        pltpu.VMEM((span, columns), jnp.float32),
        pltpu.VMEM((span, columns), jnp.float32),
        pltpu.VMEM((rows, 128), jnp.float32),
        pltpu.VMEM((rows, 128), jnp.float32),
    ]
    if first:
        outs += [
            jax.ShapeDtypeStruct((4, LO, X, features, columns), jnp.bfloat16),
            jax.ShapeDtypeStruct((4, 1, columns), jnp.float32),
        ]
    else:
        buffers = [pltpu.VMEM((16, 128), jnp.float32)] * 2 + buffers
    operands = (*texts, *operands)
    return pl.pallas_call(
        functools.partial(pair_kernel, texts=len(texts), first=first),
        in_specs=[SMEM] * 3 + [VMEM] * len(operands),
        out_specs=[VMEM] * len(outs),
        out_shape=outs,
        scratch_shapes=buffers,
        compiler_params=pltpu.CompilerParams(vmem_limit_bytes=24 * 1024 * 1024),
        cost_estimate=pl.CostEstimate(
            flops=8 * rows * columns * depth,
            bytes_accessed=2 * depth * (rows + 4 * columns),
            transcendentals=8 * rows * columns,
        ),
    )(sharpness, offsets, place, *operands)


def spread_kernel(place, keep_ref, got_ref, out_ref):
    narrow, hi, core, z = place[0], place[1], place[2], place[3]
    y = hi * 2 + narrow // X
    out_ref[...] = jnp.zeros_like(out_ref)

    @pl.when(core == 0)
    def _():
        for model, ref in enumerate((keep_ref, got_ref)):
            for dy in range(HI * LO):
                for x in range(X):
                    row, lanes = dy * 4 + x // 2, slice(x % 2 * 64, x % 2 * 64 + 64)
                    out_ref[(y ^ dy) * X + x, model : model + 1, :] = jnp.concatenate(
                        [ref[row : row + 1, lanes], ref[row + 2 : row + 3, lanes]], axis=1
                    )

    @pl.when(core == 1)
    def _():
        for model, ref in enumerate((keep_ref, got_ref)):
            for planes in range(Z):
                row = planes // 2 * 4 + planes % 2
                to = lax.rem(z + Z - planes, Z)
                out_ref[to * HI + hi, model : model + 1, :] = ref[row : row + 1, :]


def last_kernel(place, mine_ref, got_ref, image_ref, text_ref):
    mine, got = jnp.sum(mine_ref[...], axis=0), jnp.sum(got_ref[...], axis=0)

    @pl.when(place[2] == 0)
    def _():
        image_ref[...] = mine[:, :64]
        text_ref[0:1, :] = got[1:2, :64]
        text_ref[1:2, :] = got[0:1, :64]

    @pl.when(place[2] == 1)
    def _():
        image_ref[...] = got[:, 64:]
        text_ref[0:1, :] = mine[1:2, 64:]
        text_ref[1:2, :] = mine[0:1, 64:]


def reduce_sums(place, keep, give):
    def part(*shape):
        return jax.ShapeDtypeStruct(shape, jnp.float32)

    def call(kernel, specs, outs, *operands):
        return pl.pallas_call(
            kernel,
            in_specs=specs,
            out_specs=[VMEM] * len(outs),
            out_shape=outs,
            compiler_params=SMALL,
        )(*operands)

    groups = groups_by(
        lambda hi, z, c, lo, x: (c, lo, x) if c else (c, z, 0),
        lambda hi, z, c, lo, x: (z, hi) if c else (hi, lo, x),
    )
    chunks = HI * LO * X
    (sums,) = call(
        spread_kernel, [SMEM, VMEM, VMEM], [part(chunks, 2, 128)], place, keep, send_core(give)
    )
    mine = exchange(sums, groups)
    got = send_core(mine)
    return call(last_kernel, [SMEM, VMEM, VMEM], [part(2, 64)] * 2, place, mine, got)


def on_device(
    student_picture_vectors,
    student_caption_vectors,
    teacher_picture_vectors,
    teacher_caption_vectors,
    sharpness_factors,
    offset_couple,
):
    features = student_picture_vectors.shape[0]
    narrow = lax.axis_index("narrow")
    wide = lax.axis_index("wide")
    core = wide % CORES
    place = jnp.stack([narrow, wide // (Z * CORES), core, wide // CORES % Z]).astype(jnp.int32)
    learner = core == 0

    pictures = jnp.where(learner, teacher_picture_vectors, student_picture_vectors)
    other_pictures = send_core(pictures)
    shares = text_shares(student_caption_vectors, teacher_caption_vectors)
    both = jnp.where(
        learner,
        jnp.stack([student_picture_vectors, other_pictures]),
        jnp.stack([other_pictures, teacher_picture_vectors]),
    )
    both, shares = lax.optimization_barrier((both, shares))
    ring = [both] + [send_first(both, d) for d in (1, 2, 3)]

    by_row = groups_by(lambda hi, z, c, lo, x: (hi, z), lambda hi, z, c, lo, x: (c, lo, x))
    text = text_rows(place, exchange(shares, by_row), features)
    _, *ring = lax.optimization_barrier((text, *ring))
    line = jnp.stack(ring)
    one, three = send_second(line, 1), send_second(line, 3)
    two_low, two_high = send_second(three[:2], 1), send_second(one[2:], 3)

    up1, down1 = send_z(text, 1), send_z(text, -1)
    up2, down2 = send_z(up1, 1), send_z(down1, -1)
    up3, down3 = send_z(up2, 1), send_z(down2, -1)
    down4 = send_z(down3, -1)

    scalars = (sharpness_factors, offset_couple, place)
    image_sums, text_sums, image, scale = pair_sums(
        *scalars, (text, up1, down1, up2, down2), (line, one, two_low, two_high, three), True
    )
    keep, give = pair_sums(
        *scalars, (up3, down3, down4), (image, scale, image_sums, text_sums), False
    )
    return tuple(reduce_sums(place, keep, give))


def solution(mesh):
    return jax.shard_map(
        on_device,
        mesh=mesh,
        in_specs=(
            P("narrow", "wide"),
            P("narrow", "wide"),
            P("narrow", "wide"),
            P("narrow", "wide"),
            P(),
            P(),
        ),
        out_specs=(P(None, ("wide", "narrow")), P(None, ("wide", "narrow"))),
        check_vma=False,
    )
```
